512 devices in a mesh: ctx: 32 (over z, x_lo), exp: 8 (over x_hi, y), rep: 2 (over core).
Axes of the slice: x: 4 (x_hi: 2, x_lo: 2; x = x_hi * 2 + x_lo), y: 4, z: 16, core: 2. Of those that a mesh axis runs over, the one named last changes fastest.
Arguments:
- queries: bfloat16 [2, 4096, 8, 512], P('rep', 'ctx', 'exp'), may hold values from -36 to 36
- latents: bfloat16 [2, 4096, 512], P('rep', 'ctx'), may hold values from -6 to 6
- tokens: bfloat16 [2, 4096, 2048], P('rep', 'ctx', 'exp'), may hold values from -12 to 12
- block_mask: int32 [8, 32, 32], P('exp'), may hold values 0 or 1
- uv_weight: bfloat16 [8, 512, 128], P('exp'), may hold values from -0.25 to 0.25
- out_weight: bfloat16 [8, 128, 2048], P('exp'), may hold values from -0.5 to 0.5
- norm_gain: bfloat16 [2048], P('exp'), may hold values from 0.099609375 to 1.8984375
- router_matrix: bfloat16 [64, 2048], P(None, 'exp'), may hold values from -0.25 to 0.25
- routes: int32 [2, 4096, 6], P('rep', 'ctx'), may hold values from 0 to 63, all different within a row; in each aligned block of 128 rows (0 to 127, 128 to 255, ..., all dimensions but the last counted through in order) at most 16 rows name the same one
- gate_weight: bfloat16 [64, 1408, 2048], P(('ctx', 'rep'), 'exp'), may hold values from -0.125 to 0.125
- up_weight: bfloat16 [64, 1408, 2048], P(('ctx', 'rep'), 'exp'), may hold values from -0.125 to 0.125
- down_weight: bfloat16 [64, 1408, 2048], P(('ctx', 'rep'), None, 'exp'), may hold values from -0.15625 to 0.15625
Outputs:
- hidden: bfloat16 [2, 4096, 2048], P('rep', 'ctx', 'exp')
- routed: bfloat16 [2, 4096, 2048], P('rep', 'ctx', 'exp')
The draws below stay inside these ranges and needn't reach their ends.
Inputs may be any that keep to these rules, and one draw needn't show every extreme that they name: `routes`: in each aligned block of 128 tokens (one sequence's positions on one index of ctx) no expert is named more than 16 times, a bound that some block reaches; the 6 experts of a token differ.
All inputs are finite; a program needn't handle non-finite values. No bound on the sum of `block_mask` on one device may be relied on, other than what follows from the above.
Results may differ from the reference program's by a relative error of at most 0.029.
Values may be sent and summed in bfloat16 or wider, within the bound.
No kernel may reach another device: no remote copies, remote signals or barrier semaphores. Data moves between devices by JAX's collectives and lax.ppermute only.
A program may use at most 64 MiB of HBM per device.

```python
import math
import jax
import jax.numpy as jnp
import numpy as np
from jax import lax

D = 2048
LAT = 512
DV = 128
HEADS = 8
FF = 1408
TOP = 6
S_DEV = 128
E = 64
CAP = 16
SEQS = 2
SEQLEN = 4096
N_CTX = 32


def shared_latents(key):
    return jnp.clip(jax.random.normal(key, (SEQS, SEQLEN, LAT), jnp.float32), -6.0, 6.0)


def draw_latents(key, part):
    base = shared_latents(key)
    return base.astype(jnp.bfloat16)


def draw_queries(key, part):
    key = jax.random.fold_in(key, 23)
    noise = 0.7 * jnp.clip(jax.random.normal(key, (SEQS, SEQLEN, HEADS, LAT), jnp.float32), -6.0, 6.0)
    return noise.astype(jnp.bfloat16)


def draw_tokens(key, part):
    key = jax.random.fold_in(key, 37)
    key_base, key_rows, key_cols = jax.random.split(key, 3)
    shape = (SEQS, SEQLEN, D)
    base = jnp.clip(jax.random.normal(key_base, shape, jnp.float32), -6.0, 6.0)
    row_scale = jnp.exp(jax.random.uniform(key_rows, (SEQS, SEQLEN, 1), jnp.float32, 0.0, math.log(10.0)))
    col_scale = jnp.exp(jax.random.uniform(key_cols, (1, 1, D), jnp.float32, 0.0, math.log(10.0)))
    return (0.02 * base * row_scale * col_scale).astype(jnp.bfloat16)


def with_ends(entries, key, smallest, high):
    extent = entries.shape
    index_at = [jax.random.randint(jax.random.fold_in(key, axis), (), 0, extent[axis]) for axis in range(len(extent))]
    entries = entries.at[tuple(index_at)].set(smallest)
    longest = extent.index(max(extent))
    index_at[longest] = (index_at[longest] + 1) % extent[longest]
    return entries.at[tuple(index_at)].set(high)


def block_scale(stream_key, extent, shards, least, high):
    loudness = 1.0
    for axis_at, parts in shards:
        heights = jax.random.uniform(jax.random.fold_in(jax.random.fold_in(stream_key, 6), axis_at), (parts,), jnp.float32, least / len(shards), high / len(shards))
        loudness = loudness * jnp.repeat(jnp.exp(heights), extent[axis_at] // parts).reshape((-1,) + (1,) * (len(extent) - 1 - axis_at))
    return loudness


def routed_block(key, own, number, rows, number_of, top, bound, lean):
    sequence = jax.random.permutation(key, number_of)
    heavy_load, usual = load_shares(number_of, rows * top, bound, lean, True), load_shares(number_of, rows * top, bound, lean, False)
    places = jnp.arange(number_of)

    def named(tallies, offset_by):
        used = int((tallies > 0).sum())
        fixed = max(1, used // 4)
        passed = fixed + (places - fixed + offset_by * (used - fixed)) % max(1, number_of - fixed)
        return jnp.zeros((number_of,), jnp.int32).at[sequence[jnp.where(places < fixed, places, passed)]].set(jnp.asarray(tallies, jnp.int32))

    tallies = jnp.where(number % 4 == 0, named(heavy_load, number // 4), named(usual, number - number // 4 - 1))
    mixed = jax.random.permutation(jax.random.fold_in(own, 3), number_of)
    donor, sink = mixed[0:number_of // 2 * 2:2], mixed[1:number_of // 2 * 2:2]
    room = jnp.minimum(tallies[donor] - 1, bound - tallies[sink]) // 2
    room = jnp.where((donor == sequence[0]) | (sink == sequence[0]) | (tallies[sink] == 0), 0, jnp.maximum(room, 0))
    passed = jax.random.randint(jax.random.fold_in(own, 4), (number_of // 2,), 0, 1 << 20) % (room + 1)
    tallies = tallies.at[donor].add(-passed).at[sink].add(passed)
    items = jnp.searchsorted(jnp.cumsum(tallies), jnp.arange(rows * top), side="right").astype(jnp.int32)
    grid = items.reshape(top, rows).T
    grid = grid[jax.random.permutation(jax.random.fold_in(own, 1), rows)]
    offset_by = jax.random.randint(jax.random.fold_in(own, 2), (rows, 1), 0, top)
    return jnp.take_along_axis(grid, (jnp.arange(top)[None, :] + offset_by) % top, axis=1)


def load_shares(count, total, reach, slope, full):
    weights = [(1 << 20) // math.isqrt(standing ** slope) + 1 for standing in range(1, count + 1)]
    largest = reach if full else min(reach, max(-(-total // count), total * weights[0] // sum(weights)))
    least = 1 if total - largest >= count - 1 else 0
    counts, surplus = [largest] + [least] * (count - 1), total - largest - least * (count - 1)
    while surplus > 0:
        candidates = [i for i in range(1, count) if counts[i] < largest] or [i for i in range(1, count) if counts[i] < reach]
        whole, left = sum([weights[i] for i in candidates]), surplus
        for i in candidates:
            extra = min(reach - counts[i], max(1, left * weights[i] // whole), surplus)
            counts[i] = counts[i] + extra
            surplus = surplus - extra
    return np.array(counts)


def normal_values(rng, extent, width, bound, cuts=(), kind=jnp.bfloat16):
    drawn = jax.random.normal(rng, extent, jnp.float32) * width
    if len(cuts) > 0:
        drawn = block_scale(rng, extent, cuts, -0.22, 0.18) * drawn
    return jnp.clip(drawn, min=-bound, max=bound).astype(kind)


def setup_inputs(seed: int = 0) -> dict:
    streams_of = jax.random.split(jax.random.key(seed), 13)
    queries = draw_queries(jax.random.fold_in(streams_of[12], 71), 0)
    latents = draw_latents(jax.random.fold_in(streams_of[12], 71), 0)
    tokens = draw_tokens(jax.random.fold_in(streams_of[12], 71), 0)
    block_mask = with_ends((jax.random.randint(streams_of[3], (HEADS, N_CTX, N_CTX), 0, 4) < 1).astype(jnp.int32), jax.random.fold_in(streams_of[3], 1), 0, 1)
    uv_weight = normal_values(streams_of[4], (HEADS, LAT, DV), LAT ** -0.5, 0.25, ((0, 8),))
    out_weight = normal_values(streams_of[5], (HEADS, DV, D), (DV * HEADS // 8) ** -0.5, 0.5, ((0, 8),))
    norm_gain = jnp.clip(1.0 + 0.18 * jax.random.normal(streams_of[6], (D,), jnp.float32), 0.099609375, 1.8984375).astype(jnp.bfloat16)
    router_matrix = normal_values(streams_of[7], (E, D), (D // 4) ** -0.5, 0.25, ((1, 8),))
    routes_keys = jax.random.split(jax.random.fold_in(streams_of[8], 1), SEQS * SEQLEN // S_DEV)
    routes_turns = jax.random.permutation(jax.random.fold_in(streams_of[8], 3), SEQS * SEQLEN // S_DEV)
    routes = jax.vmap(lambda own, number: routed_block(jax.random.fold_in(streams_of[8], 2), own, number, S_DEV, E, TOP, CAP, 1))(routes_keys, routes_turns).reshape((SEQS, SEQLEN, TOP))
    gate_weight = normal_values(streams_of[9], (E, FF, D), D ** -0.5, 0.125, ((0, 64), (1, 8)))
    up_weight = normal_values(streams_of[10], (E, FF, D), D ** -0.5, 0.125, ((0, 64), (1, 8)))
    down_weight = normal_values(streams_of[11], (E, FF, D), FF ** -0.5, 0.15625, ((0, 64), (2, 8)))
    return dict(queries=queries, latents=latents, tokens=tokens, block_mask=block_mask, uv_weight=uv_weight, out_weight=out_weight, norm_gain=norm_gain, router_matrix=router_matrix, routes=routes, gate_weight=gate_weight, up_weight=up_weight, down_weight=down_weight)


score_scale = 192.0 ** (-0.5)
epsilon = 1e-06

def attend_sequence(query_seq, latent_seq, block_mask, uv_weight, out_weight):
    positions = jnp.arange(SEQLEN, dtype=jnp.int32)
    blocks = positions // S_DEV
    same_block = (blocks[:, None] == blocks[None, :]) & (positions[None, :] <= positions[:, None])
    earlier = blocks[None, :] < blocks[:, None]
    latent_wide = latent_seq.astype(jnp.float32)

    def head_step(total, head_index):
        query_head = lax.dynamic_index_in_dim(query_seq, head_index, 1, keepdims=False)
        mask_head = lax.dynamic_index_in_dim(block_mask, head_index, 0, keepdims=False)
        chosen = mask_head[blocks[:, None], blocks[None, :]]
        allowed = same_block | earlier & (chosen == 1)
        scores = jnp.dot(query_head.astype(jnp.float32), latent_wide.T, precision=lax.Precision.HIGHEST) * score_scale
        scores = jnp.where(allowed, scores, -jnp.inf)
        highest = lax.optimization_barrier(jnp.max(scores, axis=1, keepdims=True))
        probs = jnp.where(allowed, jnp.exp(scores - highest), 0.0)
        denom = lax.optimization_barrier(jnp.sum(probs, axis=1, keepdims=True))
        probs_low = probs.astype(jnp.bfloat16)
        latent_out = (jnp.dot(probs_low.astype(jnp.float32), latent_wide, precision=lax.Precision.HIGHEST) / denom).astype(jnp.bfloat16)
        uv_head = lax.dynamic_index_in_dim(uv_weight, head_index, 0, keepdims=False)
        out_head = lax.dynamic_index_in_dim(out_weight, head_index, 0, keepdims=False)
        head_values = jnp.dot(latent_out.astype(jnp.float32), uv_head.astype(jnp.float32), precision=lax.Precision.HIGHEST).astype(jnp.bfloat16)
        term = jnp.dot(head_values.astype(jnp.float32), out_head.astype(jnp.float32), precision=lax.Precision.HIGHEST)
        return (total + term, None)
    start = jnp.zeros((SEQLEN, D), jnp.float32)
    total, unused = lax.scan(head_step, start, jnp.arange(HEADS, dtype=jnp.int32))
    return total

def reference(queries, latents, tokens, block_mask, uv_weight, out_weight, norm_gain, router_matrix, routes, gate_weight, up_weight, down_weight):
    attention = jnp.stack([attend_sequence(queries[seq_index], latents[seq_index], block_mask, uv_weight, out_weight) for seq_index in range(SEQS)])
    hidden = (tokens.astype(jnp.float32) + attention).astype(jnp.bfloat16)
    expanded_hidden = hidden.astype(jnp.float32)
    mean_square = lax.optimization_barrier(jnp.mean(expanded_hidden * expanded_hidden, axis=-1))
    inverse_root_mean = lax.rsqrt(mean_square + epsilon)
    rescaled_rows = expanded_hidden * norm_gain.astype(jnp.float32)
    normed = (rescaled_rows * inverse_root_mean[..., None]).astype(jnp.bfloat16)
    router_scores = inverse_root_mean[..., None] * jnp.einsum('yqj,mj->yqm', rescaled_rows, router_matrix.astype(jnp.float32), precision=lax.Precision.HIGHEST)
    all_tokens = SEQS * SEQLEN
    groups = all_tokens // S_DEV
    flat_logits = router_scores.reshape(all_tokens, E)
    flat_routes = routes.reshape(all_tokens, TOP)
    picked = jnp.take_along_axis(flat_logits, flat_routes, axis=1)
    gates = jax.nn.sigmoid(picked)
    route_weight = gates / lax.optimization_barrier(jnp.sum(gates, axis=1, keepdims=True))
    grouped = flat_routes.reshape(groups, S_DEV * TOP)
    onehot = (grouped[..., None] == jnp.arange(E, dtype=jnp.int32)).astype(jnp.int32)
    slot = lax.optimization_barrier(jnp.sum(onehot * (jnp.cumsum(onehot, axis=1) - 1), axis=-1)).astype(jnp.int32)
    group_ids = jnp.arange(groups, dtype=jnp.int32)[:, None]
    place = (grouped * (groups * CAP) + group_ids * CAP + slot).astype(jnp.int32)
    token_ids = (group_ids * S_DEV + jnp.arange(S_DEV * TOP, dtype=jnp.int32)[None, :] // TOP).astype(jnp.int32)
    token_lookup = jnp.zeros((E * groups * CAP,), jnp.int32).at[place.reshape(-1)].set(token_ids.reshape(-1))
    filled = jnp.zeros((E * groups * CAP,), jnp.int32).at[place.reshape(-1)].set(1)
    normed_flat = normed.reshape(all_tokens, D)

    def expert_step(expert_index):
        begin = (expert_index * groups * CAP).astype(jnp.int32)
        index_rows = lax.dynamic_slice_in_dim(token_lookup, begin, groups * CAP)
        used = lax.dynamic_slice_in_dim(filled, begin, groups * CAP)
        gate_in = jnp.where(used[:, None] == 1, normed_flat[index_rows], jnp.zeros((), jnp.bfloat16))
        gate_rows = lax.dynamic_index_in_dim(gate_weight, expert_index, 0, keepdims=False)
        up_rows = lax.dynamic_index_in_dim(up_weight, expert_index, 0, keepdims=False)
        down_rows = lax.dynamic_index_in_dim(down_weight, expert_index, 0, keepdims=False)
        gate_proj = jnp.dot(gate_in, gate_rows.T, preferred_element_type=jnp.float32)
        up_proj = jnp.dot(gate_in, up_rows.T, preferred_element_type=jnp.float32)
        activation = (jax.nn.silu(gate_proj) * up_proj).astype(jnp.bfloat16)
        return jnp.dot(activation, down_rows, preferred_element_type=jnp.float32).astype(jnp.bfloat16)
    expert_out = lax.map(expert_step, jnp.arange(E, dtype=jnp.int32)).reshape(E * groups * CAP, D)
    place_tok = place.reshape(all_tokens, TOP)
    routed = jnp.zeros((all_tokens, D), jnp.float32)
    for routing_index in range(TOP):
        values = expert_out[place_tok[:, routing_index]].astype(jnp.float32)
        routed = routed + route_weight[:, routing_index:routing_index + 1] * values
    routed = routed.astype(jnp.bfloat16).reshape(SEQS, SEQLEN, D)
    return (hidden, routed)
```

```python
import jax
import jax.numpy as jnp
from jax import lax
from jax.experimental import pallas as pl
from jax.experimental.pallas import tpu as pltpu
from jax.sharding import Mesh, PartitionSpec as P

score_scale = 192.0 ** (-0.5)
epsilon = 1e-06
never = 1 << 20

f32 = jnp.float32
bf16 = jnp.bfloat16

in_vmem = pl.BlockSpec(memory_space=pltpu.VMEM)
in_smem = pl.BlockSpec(memory_space=pltpu.SMEM)


def iota(shape, dim):
    return lax.broadcasted_iota(jnp.int32, shape, dim)


def dot(a, b, ca, cb, **kw):
    return lax.dot_general(a, b, (((ca,), (cb,)), ((), ())), preferred_element_type=f32, **kw)


def call(kernel, outs, *operands, specs=None, scratch=(), limit=24):
    many = isinstance(outs, list)
    return pl.pallas_call(
        kernel,
        out_shape=outs,
        in_specs=specs or [in_vmem] * len(operands),
        out_specs=[in_vmem] * len(outs) if many else in_vmem,
        scratch_shapes=list(scratch),
        compiler_params=pltpu.CompilerParams(vmem_limit_bytes=limit << 20),
    )(*operands)


def membership(routes, experts):
    lane = iota((routes.shape[0], experts), 1)
    member = routes[:, 0:1] == lane
    for k in range(1, routes.shape[1]):
        member = member | (routes[:, k : k + 1] == lane)
    return member


def repeat_matrix(experts, capacity):
    wide = (experts, experts * capacity)
    return (iota(wide, 1) // capacity == iota(wide, 0)).astype(f32).astype(bf16)


def place_kernel(experts, capacity, routes_ref, place_ref):
    rows = routes_ref.shape[0]
    member = membership(routes_ref[...], experts)
    earlier = (iota((rows, rows), 1) < iota((rows, rows), 0)).astype(f32).astype(bf16)
    count = dot(earlier, member.astype(f32).astype(bf16), 1, 0)
    code = jnp.where(member, count, -1.0).astype(bf16)
    spread = dot(code, repeat_matrix(experts, capacity), 1, 0)
    slot = iota((rows, experts * capacity), 1) % capacity
    place_ref[...] = (spread == slot.astype(f32)).astype(f32).astype(bf16)


def attend_kernel(rows, part_rows, at_ref, query_ref, key_ref, out_ref):
    own_block, own_part = at_ref[0], at_ref[1]
    heads = query_ref.shape[0]
    keys = key_ref[...]
    count = keys.shape[0]
    lane = iota((count, 128), 1)
    block = iota((count, 128), 0) // part_rows
    earlier = ((block == lane) & (lane < own_block)).astype(f32).astype(bf16)
    key_row = iota((count, 1), 0)
    is_own = key_row // part_rows == own_block
    own_pos = own_part * part_rows + key_row % part_rows
    query_pos = iota((count, rows), 1)
    for h in range(heads):
        chosen = dot(earlier, query_ref[h, rows : rows + 16, 256:384], 1, 1)[:, 0:1]
        first = jnp.where(is_own, own_pos, jnp.where(chosen > 0.5, -1, never))
        allowed = first <= query_pos
        scores = dot(keys, query_ref[h, 0:rows, :], 1, 1) * score_scale
        scores = jnp.where(allowed, scores, -1e30)
        top = jnp.max(scores, axis=0, keepdims=True)
        probs = jnp.where(allowed, jnp.exp(scores - top), 0.0)
        total = jnp.sum(probs, axis=0, keepdims=True)
        some = total > 0.0
        scale = jnp.where(some, 1.0 / jnp.where(some, total, 1.0), 0.0)
        low = (probs * scale).astype(bf16)
        out_ref[h, 0:rows, :] = dot(low, keys, 0, 0).astype(bf16)
        level = jnp.where(some, top + jnp.log(jnp.where(some, total, 1.0)), -1e30)
        high = level.astype(bf16).astype(f32)
        middle = (level - high).astype(bf16).astype(f32)
        rest = level - high - middle
        at = iota((16, rows), 0)
        stats = jnp.where(at == 0, high, jnp.where(at == 1, middle, jnp.where(at == 2, rest, 0.0)))
        out_ref[h, rows : rows + 16, 0:rows] = stats.astype(bf16)
        out_ref[h, rows : rows + 16, rows:] = jnp.zeros((16, keys.shape[1] - rows), bf16)


def project_kernel(rows, part_ref, uv_ref, out_weight_ref, out_ref):
    parts = part_ref.shape[0]
    levels = []
    for s in range(parts):
        stats = part_ref[s, rows : rows + 16, 0:rows].astype(f32)
        levels.append(stats[0:1] + stats[1:2] + stats[2:3])
    top = levels[0]
    for level in levels[1:]:
        top = jnp.maximum(top, level)
    shares = [jnp.exp(level - top) for level in levels]
    total = shares[0]
    for share in shares[1:]:
        total = total + share
    scale = 1.0 / total
    at = iota((rows, rows), 0)
    square = jnp.zeros((rows, rows), f32)
    for s in range(parts):
        square = jnp.where(at == s, shares[s] * scale, square)
    columns = square.T
    latent = columns[:, 0:1] * part_ref[0, 0:rows, :].astype(f32)
    for s in range(1, parts):
        latent = latent + columns[:, s : s + 1] * part_ref[s, 0:rows, :].astype(f32)
    values = dot(latent.astype(bf16), uv_ref[...], 1, 0).astype(bf16)
    width = out_ref.shape[2]
    for d in range(out_ref.shape[0]):
        out_ref[d] = dot(values, out_weight_ref[:, d * width : (d + 1) * width], 1, 0).astype(bf16)


def hidden_kernel(
    part_ref, token_ref, place_ref, router_ref, gain_ref, hidden_ref, rows_ref, logit_ref
):
    attention = part_ref[0].astype(f32)
    for s in range(1, part_ref.shape[0]):
        attention = attention + part_ref[s].astype(f32)
    hidden = (token_ref[...].astype(f32) + attention).astype(bf16)
    hidden_ref[...] = hidden
    rows_ref[...] = dot(place_ref[...], hidden, 0, 0).astype(bf16)
    wide = hidden.astype(f32)
    experts, width = router_ref.shape
    lanes = logit_ref.shape[1]
    router = jnp.concatenate(
        [router_ref[...].astype(f32), jnp.zeros((lanes - experts, width), f32)], axis=0
    )
    logits = dot(wide * gain_ref[...].astype(f32), router, 1, 1, precision=lax.Precision.HIGHEST)
    squares = jnp.sum(wide * wide, axis=1, keepdims=True)
    logit_ref[...] = jnp.where(iota(logits.shape, 1) < experts, logits, squares)


def gate_kernel(rows_ref, gain_ref, gate_ref, up_ref, out_ref, normed_ref):
    parts, count, width = rows_ref.shape
    squares = jnp.zeros((count, 1), f32)
    for s in range(parts):
        wide = rows_ref[s].astype(f32)
        squares = squares + jnp.sum(wide * wide, axis=1, keepdims=True)
    inverse = lax.rsqrt(squares / (parts * width) + epsilon)
    for s in range(parts):
        scaled = rows_ref[s].astype(f32) * gain_ref[s].astype(f32)
        normed_ref[:, s * width : (s + 1) * width] = (scaled * inverse).astype(bf16)
    units = gate_ref.shape[1]
    for j in range(gate_ref.shape[0]):
        gate = dot(gate_ref[j], normed_ref[...], 1, 1)
        up = dot(up_ref[j], normed_ref[...], 1, 1)
        out_ref[j * units : (j + 1) * units, :] = (gate / (1.0 + jnp.exp(-gate)) * up).astype(bf16)


def down_kernel(act_ref, down_ref, out_ref):
    act = act_ref[...]
    for j in range(down_ref.shape[0]):
        out_ref[j] = dot(act, down_ref[j], 0, 0).astype(bf16)


def combine_kernel(experts, capacity, features, logit_ref, routes_ref, place_ref, back_ref, out_ref):
    total = logit_ref[0]
    for s in range(1, logit_ref.shape[0]):
        total = total + logit_ref[s]
    inverse = lax.rsqrt(total[:, experts : experts + 1] / features + epsilon)
    gates = 1.0 / (1.0 + jnp.exp(-(inverse * total[:, 0:experts])))
    gates = jnp.where(membership(routes_ref[...], experts), gates, 0.0)
    weight = gates / jnp.sum(gates, axis=1, keepdims=True)
    high = weight.astype(bf16)
    low = (weight - high.astype(f32)).astype(bf16)
    spread = repeat_matrix(experts, capacity)
    place = place_ref[...].astype(f32)
    back = back_ref[...]
    first = dot((dot(high, spread, 1, 0) * place).astype(bf16), back, 1, 0)
    second = dot((dot(low, spread, 1, 0) * place).astype(bf16), back, 1, 0)
    out_ref[...] = (first + second).astype(bf16)


def shape(*dims, dtype=bf16):
    return jax.ShapeDtypeStruct(dims, dtype)


def swap(x, axes):
    return lax.all_to_all(x, axes, split_axis=0, concat_axis=0, tiled=True)


def copies(x, n):
    return jnp.broadcast_to(x[None], (n,) + x.shape)


CTX, EXP = ("z", "xl"), ("xh", "y")


def body(
    queries,
    latents,
    tokens,
    block_mask,
    uv_weight,
    out_weight,
    norm_gain,
    router_matrix,
    routes,
    gate_weight,
    up_weight,
    down_weight,
):
    rows, latent_width = queries.shape[1], queries.shape[3]
    width = tokens.shape[2]
    experts = router_matrix.shape[0]
    capacity = 4 * rows * routes.shape[2] // (3 * experts)
    blocks = block_mask.shape[1]
    n_exp = lax.axis_size(EXP)
    n_y, n_xh = lax.axis_size("y"), lax.axis_size("xh")
    ctx_place, exp_place = lax.axis_index(CTX), lax.axis_index(EXP)
    part_rows = rows // n_exp
    features = width * n_exp
    slots = experts * capacity
    units = gate_weight.shape[1]

    mask_row = lax.dynamic_index_in_dim(block_mask[0], ctx_place, 0, keepdims=True)
    extra = jnp.concatenate(
        [
            norm_gain[None, :],
            mask_row.astype(bf16),
            jnp.zeros((1, latent_width - width - blocks), bf16),
        ],
        axis=1,
    )
    sent = jnp.concatenate([queries[0, :, 0, :], extra, jnp.zeros((15, latent_width), bf16)], axis=0)
    own_keys = lax.dynamic_slice_in_dim(latents[0], exp_place * part_rows, part_rows, 0)
    keys = swap(copies(own_keys, blocks), CTX).reshape(blocks * part_rows, latent_width)
    all_queries = swap(copies(sent, n_exp), EXP)

    gate_rows = lax.all_gather(gate_weight[0], "y")
    up_rows = lax.all_gather(up_weight[0], "y")
    down_rows = lax.all_gather(down_weight[0], "y")

    place = call(
        lambda *refs: place_kernel(experts, capacity, *refs), shape(rows, slots), routes[0]
    )
    partial = call(
        lambda *refs: attend_kernel(rows, part_rows, *refs),
        shape(n_exp, rows + 16, latent_width),
        jnp.stack([ctx_place, exp_place]).astype(jnp.int32),
        all_queries,
        keys,
        specs=[in_smem, in_vmem, in_vmem],
    )
    partial = swap(partial, EXP)
    terms = call(
        lambda *refs: project_kernel(rows, *refs),
        shape(n_exp, rows, width),
        partial,
        uv_weight[0],
        out_weight[0],
    )
    terms = swap(terms, EXP)
    hidden, picked, logits = call(
        hidden_kernel,
        [shape(rows, width), shape(slots, width), shape(rows, 128, dtype=f32)],
        terms,
        tokens[0],
        place,
        router_matrix,
        norm_gain[None, :],
    )
    received = swap(picked.reshape(experts, capacity, width), CTX + ("rep",))
    logits = swap(copies(logits, n_exp), EXP)
    groups = received.reshape(1, n_y, slots // n_y, width)
    groups = jnp.broadcast_to(groups, (n_xh,) + groups.shape[1:]).reshape(n_exp, -1, width)
    full_rows = swap(groups, EXP)
    gains = all_queries[:, rows : rows + 1, 0:width]
    count = slots // n_y
    act = call(
        gate_kernel,
        shape(n_y * units, count),
        full_rows,
        gains,
        gate_rows,
        up_rows,
        scratch=[pltpu.VMEM((count, features), bf16)],
    )
    act = swap(copies(act, n_xh), "xh").reshape(n_exp * units, count)
    out = call(down_kernel, shape(n_y, count, width), act, down_rows)
    out = swap(out, "y")
    back = swap(out.reshape(experts, capacity, width), CTX + ("rep",)).reshape(slots, width)
    routed = call(
        lambda *refs: combine_kernel(experts, capacity, features, *refs),
        shape(rows, width),
        logits,
        routes[0],
        place,
        back,
    )
    return (hidden[None], routed[None])


def solution(mesh):
    sizes = mesh.shape
    fine = Mesh(
        mesh.devices.reshape(sizes["ctx"] // 2, 2, 2, sizes["exp"] // 2, sizes["rep"]),
        ("z", "xl", "xh", "y", "rep"),
    )
    placed = (
        P("rep", CTX, EXP, None),
        P("rep", CTX, None),
        P("rep", CTX, EXP),
        P(EXP, None, None),
        P(EXP, None, None),
        P(EXP, None, None),
        P(EXP),
        P(None, EXP),
        P("rep", CTX, None),
        P(CTX + ("rep",), EXP, None),
        P(CTX + ("rep",), EXP, None),
        P(CTX + ("rep",), None, EXP),
    )
    return jax.shard_map(
        body,
        mesh=fine,
        in_specs=placed,
        out_specs=(P("rep", CTX, EXP), P("rep", CTX, EXP)),
        check_vma=False,
    )
```

```python
import jax
import jax.numpy as jnp
from jax import lax
from jax.experimental import pallas as pl
from jax.experimental.pallas import tpu as pltpu
from jax.sharding import Mesh, PartitionSpec as P

score_scale = 192.0 ** (-0.5)
epsilon = 1e-06
never = 1 << 20

f32 = jnp.float32
bf16 = jnp.bfloat16

in_vmem = pl.BlockSpec(memory_space=pltpu.VMEM)
in_smem = pl.BlockSpec(memory_space=pltpu.SMEM)


def iota(shape, dim):
    return lax.broadcasted_iota(jnp.int32, shape, dim)


def dot(a, b, ca, cb, **kw):
    return lax.dot_general(a, b, (((ca,), (cb,)), ((), ())), preferred_element_type=f32, **kw)


def call(kernel, outs, *operands, specs=None, limit=24):
    many = isinstance(outs, list)
    return pl.pallas_call(
        kernel,
        out_shape=outs,
        in_specs=specs or [in_vmem] * len(operands),
        out_specs=[in_vmem] * len(outs) if many else in_vmem,
        compiler_params=pltpu.CompilerParams(vmem_limit_bytes=limit << 20),
    )(*operands)


def three_terms(x):
    high = x.astype(bf16).astype(f32)
    middle = (x - high).astype(bf16).astype(f32)
    return high, middle, x - high - middle


def repeat_matrix(experts, capacity):
    tall = (experts * capacity, experts)
    return (iota(tall, 0) // capacity == iota(tall, 1)).astype(f32).astype(bf16)


def place_kernel(experts, capacity, routes_ref, place_ref):
    top, rows = routes_ref.shape
    routes = routes_ref[...]
    expert = iota((experts, rows), 0)
    member = routes[0:1] == expert
    for k in range(1, top):
        member = member | (routes[k : k + 1] == expert)
    earlier = (iota((rows, rows), 0) < iota((rows, rows), 1)).astype(f32).astype(bf16)
    count = dot(member.astype(f32).astype(bf16), earlier, 1, 0)
    code = jnp.where(member, count, -1.0).astype(bf16)
    spread = dot(repeat_matrix(experts, capacity), code, 1, 0)
    slot = iota((experts * capacity, rows), 0) % capacity
    place_ref[...] = (spread == slot.astype(f32)).astype(f32).astype(bf16)


def attend_kernel(rows, part_rows, values, at_ref, key_ref, *refs):
    query_refs, out_ref, gain_ref = refs[:-2], refs[-2], refs[-1]
    own_block, own_part, own_half, own_y = at_ref[0], at_ref[1], at_ref[2], at_ref[3]
    heads = len(query_refs)
    keys = key_ref[...]
    count = keys.shape[0]
    lane = iota((count, 128), 1)
    block = iota((count, 128), 0) // part_rows
    earlier = ((block == lane) & (lane < own_block)).astype(f32).astype(bf16)
    key_row = iota((count, 1), 0)
    is_own = key_row // part_rows == own_block
    own_pos = own_part * part_rows + key_row % part_rows
    query_pos = iota((count, rows), 1)
    width = gain_ref.shape[2]
    extra = rows + values
    n_y = heads // 2
    for n, ref in enumerate(query_refs):
        half, shift = n // n_y, n % n_y
        head = (own_half ^ half) * n_y + (own_y + n_y - shift) % n_y
        chosen = dot(earlier, ref[extra : extra + 16, width : width + 128], 1, 1)[:, 0:1]
        first = jnp.where(is_own, own_pos, jnp.where(chosen > 0.5, -1, never))
        allowed = first <= query_pos
        scores = dot(keys, ref[0:rows, :], 1, 1) * score_scale
        scores = jnp.where(allowed, scores, -1e30)
        top = jnp.max(scores, axis=0, keepdims=True)
        probs = jnp.where(allowed, jnp.exp(scores - top), 0.0)
        total = jnp.sum(probs, axis=0, keepdims=True)
        some = total > 0.0
        scale = jnp.where(some, 1.0 / jnp.where(some, total, 1.0), 0.0)
        latent = dot((probs * scale).astype(bf16), keys, 0, 0).astype(bf16)
        out_ref[head, 0:rows, :] = dot(latent, ref[rows:extra, :], 1, 1).astype(bf16)
        level = jnp.where(some, top + jnp.log(jnp.where(some, total, 1.0)), -1e30)
        terms = three_terms(level)
        at = iota((16, rows), 0)
        stats = jnp.zeros((16, rows), f32)
        for k, term in enumerate(terms):
            stats = jnp.where(at == k, term, stats)
        out_ref[head, rows : rows + 16, :] = stats.astype(bf16)
        gain_ref[head] = ref[extra : extra + 16, 0:width]


def project_kernel(rows, part_ref, out_weight_ref, out_ref):
    parts = part_ref.shape[0]
    levels = []
    for s in range(parts):
        stats = part_ref[s, rows : rows + 16, :].astype(f32)
        levels.append(stats[0:1] + stats[1:2] + stats[2:3])
    top = levels[0]
    for level in levels[1:]:
        top = jnp.maximum(top, level)
    shares = [jnp.exp(level - top) for level in levels]
    total = shares[0]
    for share in shares[1:]:
        total = total + share
    scale = 1.0 / total
    at = iota((rows, rows), 0)
    square = jnp.zeros((rows, rows), f32)
    for s in range(parts):
        square = jnp.where(at == s, shares[s] * scale, square)
    columns = square.T
    values = columns[:, 0:1] * part_ref[0, 0:rows, :].astype(f32)
    for s in range(1, parts):
        values = values + columns[:, s : s + 1] * part_ref[s, 0:rows, :].astype(f32)
    values = values.astype(bf16)
    width = out_ref.shape[2]
    for d in range(out_ref.shape[0]):
        out_ref[d] = dot(values, out_weight_ref[:, d * width : (d + 1) * width], 1, 0).astype(bf16)


def hidden_kernel(
    part_ref, token_ref, place_ref, router_ref, gain_ref, routes_ref, hidden_ref, rows_ref, pick_ref
):
    attention = part_ref[0].astype(f32)
    for s in range(1, part_ref.shape[0]):
        attention = attention + part_ref[s].astype(f32)
    hidden = (token_ref[...].astype(f32) + attention).astype(bf16)
    hidden_ref[...] = hidden
    rows_ref[...] = dot(place_ref[...], hidden, 1, 0).astype(bf16)
    wide = hidden.astype(f32)
    exact = dict(precision=lax.Precision.HIGHEST)
    scaled = wide * gain_ref[...].astype(f32)
    logits = dot(router_ref[...].astype(f32), scaled, 1, 1, **exact)
    picks = dot(jnp.ones((8, wide.shape[1]), f32), wide * wide, 1, 1, **exact)
    routes = routes_ref[...]
    expert, at = iota(logits.shape, 0), iota(picks.shape, 0)
    for k in range(routes.shape[0]):
        pick = jnp.sum(jnp.where(routes[k : k + 1] == expert, logits, 0.0), axis=0, keepdims=True)
        picks = jnp.where(at == k, pick, picks)
    high, middle, rest = three_terms(picks)
    upper = jnp.concatenate([high, middle], axis=1)
    lower = jnp.concatenate([rest, jnp.zeros_like(rest)], axis=1)
    pick_ref[...] = jnp.concatenate([upper, lower], axis=0).astype(bf16)


def gate_kernel(rows_ref, gain_ref, gate_ref, up_ref, out_ref, normed_ref):
    parts, _, width = rows_ref.shape
    count = normed_ref.shape[0]

    @pl.when(pl.program_id(0) == 0)
    def _():
        squares = jnp.zeros((count, 1), f32)
        for s in range(parts):
            wide = rows_ref[s, 0:count, :].astype(f32)
            squares = squares + jnp.sum(wide * wide, axis=1, keepdims=True)
        inverse = lax.rsqrt(squares / (parts * width) + epsilon)
        for s in range(parts):
            scaled = rows_ref[s, 0:count, :].astype(f32) * gain_ref[s, 0:1, :].astype(f32)
            normed_ref[:, s * width : (s + 1) * width] = (scaled * inverse).astype(bf16)

    gate = dot(gate_ref[0], normed_ref[...], 1, 1)
    up = dot(up_ref[0], normed_ref[...], 1, 1)
    out_ref[...] = (gate / (1.0 + jnp.exp(-gate)) * up).astype(bf16)


def down_kernel(half_ref, act_ref, down_ref, out_ref):
    width = out_ref.shape[3]
    for k in range(2):
        down = down_ref[0, :, k * width : (k + 1) * width]
        out_ref[half_ref[0] ^ k, 0] = dot(act_ref[...], down, 0, 0).astype(bf16)


def combine_kernel(experts, capacity, features, row_ref, routes_ref, place_ref, back_ref, out_ref):
    rows = out_ref.shape[0]
    count = row_ref.shape[1] - 16
    total = jnp.zeros((8, rows), f32)
    for s in range(row_ref.shape[0]):
        terms = row_ref[s, count : count + 16, :].astype(f32)
        total = total + (terms[0:8, 0:rows] + terms[0:8, rows:] + terms[8:16, 0:rows])
    routes = routes_ref[...]
    top = routes.shape[0]
    inverse = lax.rsqrt(total[top : top + 1] / features + epsilon)
    gates = 1.0 / (1.0 + jnp.exp(-(inverse * total[0:top])))
    gates = gates / jnp.sum(gates, axis=0, keepdims=True)
    expert = iota((experts, rows), 0)
    weight = jnp.zeros((experts, rows), f32)
    for k in range(top):
        weight = jnp.where(routes[k : k + 1] == expert, gates[k : k + 1], weight)
    high = weight.astype(bf16)
    low = (weight - high.astype(f32)).astype(bf16)
    spread = repeat_matrix(experts, capacity)
    place = place_ref[...].astype(f32)
    back = back_ref[...]
    first = dot((dot(spread, high, 1, 0) * place).astype(bf16), back, 0, 0)
    second = dot((dot(spread, low, 1, 0) * place).astype(bf16), back, 0, 0)
    out_ref[...] = (first + second).astype(bf16)


def shape(*dims, dtype=bf16):
    return jax.ShapeDtypeStruct(dims, dtype)


def swap(x, axes):
    return lax.all_to_all(x, axes, split_axis=0, concat_axis=0, tiled=True)


def copies(x, n):
    return jnp.broadcast_to(x[None], (n,) + x.shape)


CTX, EXP = ("z", "xl"), ("xh", "y")


def body(
    queries,
    latents,
    tokens,
    block_mask,
    uv_weight,
    out_weight,
    norm_gain,
    router_matrix,
    routes,
    gate_weight,
    up_weight,
    down_weight,
):
    rows, latent_width = queries.shape[1], queries.shape[3]
    width = tokens.shape[2]
    experts = router_matrix.shape[0]
    capacity = 4 * rows * routes.shape[2] // (3 * experts)
    blocks = block_mask.shape[1]
    values = uv_weight.shape[2]
    n_exp = lax.axis_size(EXP)
    n_y, n_xh = lax.axis_size("y"), lax.axis_size("xh")
    ctx_place, exp_place = lax.axis_index(CTX), lax.axis_index(EXP)
    half = lax.axis_index("xh")
    part_rows = rows // n_exp
    features = width * n_exp
    slots = experts * capacity
    count = slots // n_y
    units = gate_weight.shape[1]
    half_units = units * n_y

    own_keys = lax.dynamic_slice_in_dim(latents[0], exp_place * part_rows, part_rows, 0)
    keys = swap(copies(own_keys, blocks), CTX).reshape(blocks * part_rows, latent_width)
    mask_row = lax.dynamic_index_in_dim(block_mask[0], ctx_place, 0, keepdims=True)
    extra = jnp.concatenate(
        [
            norm_gain[None, :],
            mask_row.astype(bf16),
            jnp.zeros((1, latent_width - width - blocks), bf16),
        ],
        axis=1,
    )
    sent = jnp.concatenate(
        [queries[0, :, 0, :], uv_weight[0].T, extra, jnp.zeros((15, latent_width), bf16)], axis=0
    )
    all_queries = [sent]
    for n in range(1, n_exp):
        a, k = n // n_y, n % n_y
        to = [(x * n_y + y, (x ^ a) * n_y + (y + k) % n_y) for x in range(n_xh) for y in range(n_y)]
        all_queries.append(lax.ppermute(sent, EXP, to))

    gate_rows = lax.all_gather(gate_weight[0], "y")
    up_rows = lax.all_gather(up_weight[0], "y")
    down = down_weight[0]
    down_own = lax.dynamic_slice_in_dim(down, half * half_units, half_units, 0)
    down_other = lax.dynamic_slice_in_dim(down, (1 - half) * half_units, half_units, 0)
    down_other = lax.ppermute(down_other, "xh", [(0, 1), (1, 0)])
    down_rows = lax.all_gather(jnp.concatenate([down_own, down_other], axis=1), "y")

    routes_t = routes[0].T
    place = call(
        lambda *refs: place_kernel(experts, capacity, *refs), shape(slots, rows), routes_t
    )
    at = jnp.stack([ctx_place, exp_place, half, lax.axis_index("y")]).astype(jnp.int32)
    partial, gains = call(
        lambda *refs: attend_kernel(rows, part_rows, values, *refs),
        [shape(n_exp, rows + 16, values), shape(n_exp, 16, width)],
        at,
        keys,
        *all_queries,
        specs=[in_smem] + [in_vmem] * (1 + n_exp),
    )
    terms = call(
        lambda *refs: project_kernel(rows, *refs),
        shape(n_exp, rows, width),
        swap(partial, EXP),
        out_weight[0],
    )
    hidden, picked, picks = call(
        hidden_kernel,
        [shape(rows, width), shape(slots, width), shape(16, width)],
        swap(terms, EXP),
        tokens[0],
        place,
        router_matrix,
        norm_gain[None, :],
        routes_t,
    )
    received = swap(picked.reshape(experts, capacity, width), CTX + ("rep",))
    groups = jnp.concatenate(
        [received.reshape(n_y, count, width), copies(picks, n_y)], axis=1
    )
    groups = copies(groups, n_xh).reshape(n_exp, count + 16, width)
    full_rows = swap(groups, EXP)
    whole = lambda j: (0, 0, 0)
    act = pl.pallas_call(
        gate_kernel,
        grid=(n_y,),
        out_shape=shape(half_units, count),
        in_specs=[
            pl.BlockSpec((n_exp, count + 16, width), whole),
            pl.BlockSpec((n_exp, 16, width), whole),
            pl.BlockSpec((1, units, features), lambda j: (j, 0, 0)),
            pl.BlockSpec((1, units, features), lambda j: (j, 0, 0)),
        ],
        out_specs=pl.BlockSpec((units, count), lambda j: (j, 0)),
        scratch_shapes=[pltpu.VMEM((count, features), bf16)],
        compiler_params=pltpu.CompilerParams(vmem_limit_bytes=24 << 20),
    )(full_rows, gains, gate_rows, up_rows)
    out = pl.pallas_call(
        down_kernel,
        grid=(n_y,),
        out_shape=shape(n_xh, n_y, count, width),
        in_specs=[
            in_smem,
            pl.BlockSpec((half_units, count), lambda j: (0, 0)),
            pl.BlockSpec((1, half_units, n_xh * width), lambda j: (j, 0, 0)),
        ],
        out_specs=pl.BlockSpec((n_xh, 1, count, width), lambda j: (0, j, 0, 0)),
        compiler_params=pltpu.CompilerParams(vmem_limit_bytes=24 << 20),
    )(half.reshape(1).astype(jnp.int32), act, down_rows)
    out = swap(out.reshape(n_exp, count, width), EXP).reshape(n_xh, n_y, count, width)
    out = jnp.sum(out.astype(f32), axis=0).astype(bf16)
    back = swap(out.reshape(experts, capacity, width), CTX + ("rep",)).reshape(slots, width)
    routed = call(
        lambda *refs: combine_kernel(experts, capacity, features, *refs),
        shape(rows, width),
        full_rows,
        routes_t,
        place,
        back,
    )
    return (hidden[None], routed[None])


def solution(mesh):
    sizes = mesh.shape
    fine = Mesh(
        mesh.devices.reshape(sizes["ctx"] // 2, 2, 2, sizes["exp"] // 2, sizes["rep"]),
        ("z", "xl", "xh", "y", "rep"),
    )
    placed = (
        P("rep", CTX, EXP, None),
        P("rep", CTX, None),
        P("rep", CTX, EXP),
        P(EXP, None, None),
        P(EXP, None, None),
        P(EXP, None, None),
        P(EXP),
        P(None, EXP),
        P("rep", CTX, None),
        P(CTX + ("rep",), EXP, None),
        P(CTX + ("rep",), EXP, None),
        P(CTX + ("rep",), None, EXP),
    )
    return jax.shard_map(
        body,
        mesh=fine,
        in_specs=placed,
        out_specs=(P("rep", CTX, EXP), P("rep", CTX, EXP)),
        check_vma=False,
    )
```

```python
import jax
import jax.numpy as jnp
from jax import lax
from jax.experimental import pallas as pl
from jax.experimental.pallas import tpu as pltpu
from jax.sharding import Mesh, PartitionSpec as P

score_scale = 192.0 ** (-0.5)
epsilon = 1e-06
never = 1 << 20

f32 = jnp.float32
bf16 = jnp.bfloat16

in_vmem = pl.BlockSpec(memory_space=pltpu.VMEM)
in_smem = pl.BlockSpec(memory_space=pltpu.SMEM)


def iota(shape, dim):
    return lax.broadcasted_iota(jnp.int32, shape, dim)


def dot(a, b, ca, cb, **kw):
    return lax.dot_general(a, b, (((ca,), (cb,)), ((), ())), preferred_element_type=f32, **kw)


def call(kernel, outs, *operands, specs=None, scratch=(), limit=24):
    many = isinstance(outs, list)
    return pl.pallas_call(
        kernel,
        out_shape=outs,
        in_specs=specs or [in_vmem] * len(operands),
        out_specs=[in_vmem] * len(outs) if many else in_vmem,
        scratch_shapes=list(scratch),
        compiler_params=pltpu.CompilerParams(vmem_limit_bytes=limit << 20),
    )(*operands)


def three_terms(x):
    high = x.astype(bf16).astype(f32)
    middle = (x - high).astype(bf16).astype(f32)
    return high, middle, x - high - middle


def repeat_matrix(experts, capacity):
    tall = (experts * capacity, experts)
    return (iota(tall, 0) // capacity == iota(tall, 1)).astype(f32).astype(bf16)


def place_kernel(experts, capacity, routes_ref, place_ref):
    top, rows = routes_ref.shape
    routes = routes_ref[...]
    expert = iota((experts, rows), 0)
    member = routes[0:1] == expert
    for k in range(1, top):
        member = member | (routes[k : k + 1] == expert)
    earlier = (iota((rows, rows), 0) < iota((rows, rows), 1)).astype(f32).astype(bf16)
    count = dot(member.astype(f32).astype(bf16), earlier, 1, 0)
    code = jnp.where(member, count, -1.0).astype(bf16)
    spread = dot(repeat_matrix(experts, capacity), code, 1, 0)
    slot = iota((experts * capacity, rows), 0) % capacity
    place_ref[...] = (spread == slot.astype(f32)).astype(f32).astype(bf16)


def attend_kernel(rows, part_rows, at_ref, key_ref, *refs):
    pair_refs, out_ref, gain_ref = refs[:-2], refs[-2], refs[-1]
    own_block, own_part, own_half, own_y = at_ref[0], at_ref[1], at_ref[2], at_ref[3]
    n_y = len(pair_refs)
    keys = key_ref[...]
    count = keys.shape[0]
    lane = iota((count, 128), 1)
    block = iota((count, 128), 0) // part_rows
    earlier = ((block == lane) & (lane < own_block)).astype(f32).astype(bf16)
    key_row = iota((count, 1), 0)
    is_own = key_row // part_rows == own_block
    own_pos = own_part * part_rows + key_row % part_rows
    both = 2 * rows
    is_first = iota((1, both), 1) < rows
    query_pos = iota((count, both), 1) % rows
    width = gain_ref.shape[2]
    for shift in range(n_y):
        ref = pair_refs[shift]
        pair = jnp.concatenate([ref[0, 0:rows, :], ref[1, 0:rows, :]], axis=0)
        firsts = []
        for half in range(2):
            chosen = dot(earlier, ref[half, rows : rows + 16, width : width + 128], 1, 1)[:, 0:1]
            firsts.append(jnp.where(is_own, own_pos, jnp.where(chosen > 0.5, -1, never)))
        allowed = jnp.where(is_first, firsts[0], firsts[1]) <= query_pos
        scores = dot(keys, pair, 1, 1) * score_scale
        scores = jnp.where(allowed, scores, -1e30)
        top = jnp.max(scores, axis=0, keepdims=True)
        probs = jnp.where(allowed, jnp.exp(scores - top), 0.0)
        total = jnp.sum(probs, axis=0, keepdims=True)
        some = total > 0.0
        scale = jnp.where(some, 1.0 / jnp.where(some, total, 1.0), 0.0)
        latent = dot((probs * scale).astype(bf16), keys, 0, 0).astype(bf16)
        level = jnp.where(some, top + jnp.log(jnp.where(some, total, 1.0)), -1e30)
        terms = three_terms(level)
        at = iota((16, both), 0)
        stats = jnp.zeros((16, both), f32)
        for k, term in enumerate(terms):
            stats = jnp.where(at == k, term, stats)
        stats = stats.astype(bf16)
        for half in range(2):
            head = (own_half ^ half) * n_y + (own_y + n_y - shift) % n_y
            lanes = slice(half * rows, (half + 1) * rows)
            out_ref[head, 0:rows, :] = latent[lanes, :]
            out_ref[head, rows : rows + 16, 0:rows] = stats[:, lanes]
            out_ref[head, rows : rows + 16, rows:] = jnp.zeros((16, keys.shape[1] - rows), bf16)
            gain_ref[head] = ref[half, rows : rows + 16, 0:width]


def project_kernel(rows, part_ref, uv_ref, out_weight_ref, out_ref):
    parts = part_ref.shape[0]
    levels = []
    for s in range(parts):
        stats = part_ref[s, rows : rows + 16, 0:rows].astype(f32)
        levels.append(stats[0:1] + stats[1:2] + stats[2:3])
    top = levels[0]
    for level in levels[1:]:
        top = jnp.maximum(top, level)
    shares = [jnp.exp(level - top) for level in levels]
    total = shares[0]
    for share in shares[1:]:
        total = total + share
    scale = 1.0 / total
    at = iota((rows, rows), 0)
    square = jnp.zeros((rows, rows), f32)
    for s in range(parts):
        square = jnp.where(at == s, shares[s] * scale, square)
    columns = square.T
    latent = columns[:, 0:1] * part_ref[0, 0:rows, :].astype(f32)
    for s in range(1, parts):
        latent = latent + columns[:, s : s + 1] * part_ref[s, 0:rows, :].astype(f32)
    values = dot(latent.astype(bf16), uv_ref[...], 1, 0).astype(bf16)
    width = out_ref.shape[2]
    for d in range(out_ref.shape[0]):
        out_ref[d] = dot(values, out_weight_ref[:, d * width : (d + 1) * width], 1, 0).astype(bf16)


def hidden_kernel(
    part_ref, token_ref, place_ref, router_ref, gain_ref, routes_ref, hidden_ref, rows_ref, pick_ref
):
    attention = part_ref[0].astype(f32)
    for s in range(1, part_ref.shape[0]):
        attention = attention + part_ref[s].astype(f32)
    hidden = (token_ref[...].astype(f32) + attention).astype(bf16)
    hidden_ref[...] = hidden
    rows_ref[...] = dot(place_ref[...], hidden, 1, 0).astype(bf16)
    wide = hidden.astype(f32)
    exact = dict(precision=lax.Precision.HIGHEST)
    scaled = wide * gain_ref[...].astype(f32)
    logits = dot(router_ref[...].astype(f32), scaled, 1, 1, **exact)
    picks = dot(jnp.ones((8, wide.shape[1]), f32), wide * wide, 1, 1, **exact)
    routes = routes_ref[...]
    expert, at = iota(logits.shape, 0), iota(picks.shape, 0)
    for k in range(routes.shape[0]):
        pick = jnp.sum(jnp.where(routes[k : k + 1] == expert, logits, 0.0), axis=0, keepdims=True)
        picks = jnp.where(at == k, pick, picks)
    high, middle, rest = three_terms(picks)
    upper = jnp.concatenate([high, middle], axis=1)
    lower = jnp.concatenate([rest, jnp.zeros_like(rest)], axis=1)
    pick_ref[...] = jnp.concatenate([upper, lower], axis=0).astype(bf16)


def gate_kernel(at_ref, rows_ref, gain_ref, gate_ref, up_ref, gate2_ref, up2_ref, out_ref, normed_ref):
    n_y, _, width = rows_ref.shape
    count, features = normed_ref.shape
    half = at_ref[2]
    squares = jnp.zeros((count, 1), f32)
    for x in range(2):
        for y in range(n_y):
            wide = rows_ref[y, x * count : (x + 1) * count, :].astype(f32)
            squares = squares + jnp.sum(wide * wide, axis=1, keepdims=True)
    inverse = lax.rsqrt(squares / features + epsilon)
    for x in range(2):
        for y in range(n_y):
            s = x * n_y + y
            wide = rows_ref[y, x * count : (x + 1) * count, :].astype(f32)
            scaled = wide * gain_ref[s, 0:1, :].astype(f32)
            normed_ref[:, s * width : (s + 1) * width] = (scaled * inverse).astype(bf16)
    units = gate_ref.shape[0]
    for a, (g_ref, u_ref) in enumerate(((gate_ref, up_ref), (gate2_ref, up2_ref))):
        gate = dot(g_ref[...], normed_ref[...], 1, 1)
        up = dot(u_ref[...], normed_ref[...], 1, 1)
        act = (gate / (1.0 + jnp.exp(-gate)) * up).astype(bf16)
        out_ref[pl.ds(pl.multiple_of((half ^ a) * units, 16), units), :] = act


def down_kernel(at_ref, act_ref, down_ref, down2_ref, out_ref, act_all_ref):
    half = at_ref[2]
    n_y, both, _ = act_ref.shape
    units = both // 2
    for x in range(2):
        for y in range(n_y):
            at = (x * n_y + y) * units
            act_all_ref[at : at + units, :] = act_ref[y, x * units : (x + 1) * units, :]
    for a, ref in enumerate((down_ref, down2_ref)):
        out_ref[half ^ a] = dot(act_all_ref[...], ref[...], 0, 0).astype(bf16)


def combine_kernel(experts, capacity, features, row_ref, routes_ref, place_ref, back_ref, out_ref):
    rows = out_ref.shape[0]
    total = jnp.zeros((8, rows), f32)
    for s in range(row_ref.shape[0]):
        for at in range(experts * capacity, row_ref.shape[1], 16):
            terms = row_ref[s, at : at + 16, :].astype(f32)
            total = total + (terms[0:8, 0:rows] + terms[0:8, rows:] + terms[8:16, 0:rows])
    routes = routes_ref[...]
    top = routes.shape[0]
    inverse = lax.rsqrt(total[top : top + 1] / features + epsilon)
    gates = 1.0 / (1.0 + jnp.exp(-(inverse * total[0:top])))
    gates = gates / jnp.sum(gates, axis=0, keepdims=True)
    expert = iota((experts, rows), 0)
    weight = jnp.zeros((experts, rows), f32)
    for k in range(top):
        weight = jnp.where(routes[k : k + 1] == expert, gates[k : k + 1], weight)
    high = weight.astype(bf16)
    low = (weight - high.astype(f32)).astype(bf16)
    spread = repeat_matrix(experts, capacity)
    place = place_ref[...].astype(f32)
    back = back_ref[...]
    first = dot((dot(spread, high, 1, 0) * place).astype(bf16), back, 0, 0)
    second = dot((dot(spread, low, 1, 0) * place).astype(bf16), back, 0, 0)
    out_ref[...] = (first + second).astype(bf16)


def shape(*dims, dtype=bf16):
    return jax.ShapeDtypeStruct(dims, dtype)


def swap(x, axes):
    return lax.all_to_all(x, axes, split_axis=0, concat_axis=0, tiled=True)


def copies(x, n):
    return jnp.broadcast_to(x[None], (n,) + x.shape)


def all_shifts(x, n):
    turn = lambda k: [(y, (y + k) % n) for y in range(n)]
    return [x] + [lax.ppermute(x, "y", turn(k)) for k in range(1, n)]


def other_half(x):
    return lax.ppermute(x, "xh", [(0, 1), (1, 0)])


CTX, EXP = ("z", "xl"), ("xh", "y")
OWNERS = CTX + ("rep", "xh")


def body(
    queries,
    latents,
    tokens,
    block_mask,
    uv_weight,
    out_weight,
    norm_gain,
    router_matrix,
    routes,
    gate_weight,
    up_weight,
    down_weight,
):
    rows, latent_width = queries.shape[1], queries.shape[3]
    width = tokens.shape[2]
    experts = router_matrix.shape[0]
    capacity = 4 * rows * routes.shape[2] // (3 * experts)
    blocks = block_mask.shape[1]
    n_exp = lax.axis_size(EXP)
    n_y, n_xh = lax.axis_size("y"), lax.axis_size("xh")
    ctx_place, exp_place = lax.axis_index(CTX), lax.axis_index(EXP)
    half = lax.axis_index("xh")
    part_rows = rows // n_exp
    features = width * n_exp
    slots = experts * capacity
    count = slots // n_xh
    units = gate_weight.shape[1]

    own_keys = lax.dynamic_slice_in_dim(latents[0], exp_place * part_rows, part_rows, 0)
    keys = swap(copies(own_keys, blocks), CTX).reshape(blocks * part_rows, latent_width)
    mask_row = lax.dynamic_index_in_dim(block_mask[0], ctx_place, 0, keepdims=True)
    extra = jnp.concatenate(
        [
            norm_gain[None, :],
            mask_row.astype(bf16),
            jnp.zeros((1, latent_width - width - blocks), bf16),
        ],
        axis=1,
    )
    sent = jnp.concatenate(
        [queries[0, :, 0, :], extra, jnp.zeros((15, latent_width), bf16)], axis=0
    )
    all_queries = all_shifts(jnp.stack([sent, other_half(sent)]), n_y)

    gate2 = other_half(gate_weight[0])
    up2 = other_half(up_weight[0])
    down2 = other_half(down_weight[0])

    routes_t = routes[0].T
    place = call(
        lambda *refs: place_kernel(experts, capacity, *refs), shape(slots, rows), routes_t
    )
    at = jnp.stack([ctx_place, exp_place, half, lax.axis_index("y")]).astype(jnp.int32)
    partial, gains = call(
        lambda *refs: attend_kernel(rows, part_rows, *refs),
        [shape(n_exp, rows + 16, latent_width), shape(n_exp, 16, width)],
        at,
        keys,
        *all_queries,
        specs=[in_smem] + [in_vmem] * (1 + n_y),
    )
    partial = swap(partial, EXP)
    terms = call(
        lambda *refs: project_kernel(rows, *refs),
        shape(n_exp, rows, width),
        partial,
        uv_weight[0],
        out_weight[0],
    )
    terms = swap(terms, EXP)
    hidden, picked, picks = call(
        hidden_kernel,
        [shape(rows, width), shape(slots, width), shape(16, width)],
        terms,
        tokens[0],
        place,
        router_matrix,
        norm_gain[None, :],
        routes_t,
    )
    received = swap(picked.reshape(experts * n_xh, capacity // n_xh, width), OWNERS)
    received, gate2 = lax.optimization_barrier((received, gate2))
    received = received.reshape(experts, n_xh, capacity // n_xh, width).swapaxes(0, 1)
    mine = jnp.concatenate([received.reshape(slots, width), picks, other_half(picks)], axis=0)
    full_rows = swap(copies(mine, n_y), "y")
    act = call(
        gate_kernel,
        shape(n_xh * units, count),
        at,
        full_rows,
        gains,
        gate_weight[0],
        up_weight[0],
        gate2,
        up2,
        specs=[in_smem] + [in_vmem] * 6,
        scratch=[pltpu.VMEM((count, features), bf16)],
    )
    act = swap(copies(act, n_y), "y")
    out = call(
        down_kernel,
        shape(n_xh, count, width),
        at,
        act,
        down_weight[0],
        down2,
        specs=[in_smem] + [in_vmem] * 3,
        scratch=[pltpu.VMEM((n_exp * units, count), bf16)],
    )
    out = out.reshape(n_xh, experts, capacity // n_xh, width).swapaxes(0, 1)
    back = swap(out.reshape(experts * n_xh, capacity // n_xh, width), OWNERS)
    back = back.reshape(slots, width)
    routed = call(
        lambda *refs: combine_kernel(experts, capacity, features, *refs),
        shape(rows, width),
        full_rows,
        routes_t,
        place,
        back,
    )
    return (hidden[None], routed[None])


def solution(mesh):
    sizes = mesh.shape
    fine = Mesh(
        mesh.devices.reshape(sizes["ctx"] // 2, 2, 2, sizes["exp"] // 2, sizes["rep"]),
        ("z", "xl", "xh", "y", "rep"),
    )
    placed = (
        P("rep", CTX, EXP, None),
        P("rep", CTX, None),
        P("rep", CTX, EXP),
        P(EXP, None, None),
        P(EXP, None, None),
        P(EXP, None, None),
        P(EXP),
        P(None, EXP),
        P("rep", CTX, None),
        P(CTX + ("rep",), EXP, None),
        P(CTX + ("rep",), EXP, None),
        P(CTX + ("rep",), None, EXP),
    )
    return jax.shard_map(
        body,
        mesh=fine,
        in_specs=placed,
        out_specs=(P("rep", CTX, EXP), P("rep", CTX, EXP)),
        check_vma=False,
    )
```

```python
import jax
import jax.numpy as jnp
from jax import lax
from jax.experimental import pallas as pl
from jax.experimental.pallas import tpu as pltpu
from jax.sharding import Mesh, PartitionSpec as P

score_scale = 192.0 ** (-0.5)
epsilon = 1e-06
never = 1 << 20

f32 = jnp.float32
bf16 = jnp.bfloat16

in_vmem = pl.BlockSpec(memory_space=pltpu.VMEM)
in_smem = pl.BlockSpec(memory_space=pltpu.SMEM)


def iota(shape, dim):
    return lax.broadcasted_iota(jnp.int32, shape, dim)


def dot(a, b, ca, cb, **kw):
    return lax.dot_general(a, b, (((ca,), (cb,)), ((), ())), preferred_element_type=f32, **kw)


def call(kernel, outs, *operands, specs=None, scratch=(), limit=24):
    many = isinstance(outs, list)
    return pl.pallas_call(
        kernel,
        out_shape=outs,
        in_specs=specs or [in_vmem] * len(operands),
        out_specs=[in_vmem] * len(outs) if many else in_vmem,
        scratch_shapes=list(scratch),
        compiler_params=pltpu.CompilerParams(vmem_limit_bytes=limit << 20),
    )(*operands)


def three_terms(x):
    high = x.astype(bf16).astype(f32)
    middle = (x - high).astype(bf16).astype(f32)
    return high, middle, x - high - middle


def repeat_matrix(experts, capacity):
    tall = (experts * capacity, experts)
    return (iota(tall, 0) // capacity == iota(tall, 1)).astype(f32).astype(bf16)


def place_kernel(experts, capacity, routes_ref, place_ref):
    top, rows = routes_ref.shape
    routes = routes_ref[...]
    expert = iota((experts, rows), 0)
    member = routes[0:1] == expert
    for k in range(1, top):
        member = member | (routes[k : k + 1] == expert)
    earlier = (iota((rows, rows), 0) < iota((rows, rows), 1)).astype(f32).astype(bf16)
    count = dot(member.astype(f32).astype(bf16), earlier, 1, 0)
    code = jnp.where(member, count, -1.0).astype(bf16)
    spread = dot(repeat_matrix(experts, capacity), code, 1, 0)
    slot = iota((experts * capacity, rows), 0) % capacity
    place_ref[...] = (spread == slot.astype(f32)).astype(f32).astype(bf16)


def attend_kernel(rows, part_rows, at_ref, key_ref, *refs):
    pair_refs, out_ref, gain_ref = refs[:-2], refs[-2], refs[-1]
    own_block, own_part, own_half, own_y = at_ref[0], at_ref[1], at_ref[2], at_ref[3]
    n_y = len(pair_refs)
    keys = key_ref[...]
    count = keys.shape[0]
    lane = iota((count, 128), 1)
    block = iota((count, 128), 0) // part_rows
    earlier = ((block == lane) & (lane < own_block)).astype(f32).astype(bf16)
    key_row = iota((count, 1), 0)
    is_own = key_row // part_rows == own_block
    own_pos = own_part * part_rows + key_row % part_rows
    both = 2 * rows
    is_first = iota((1, both), 1) < rows
    query_pos = iota((count, both), 1) % rows
    width = gain_ref.shape[2]
    for shift in range(n_y):
        ref = pair_refs[shift]
        pair = jnp.concatenate([ref[0, 0:rows, :], ref[1, 0:rows, :]], axis=0)
        firsts = []
        for half in range(2):
            chosen = dot(earlier, ref[half, rows : rows + 16, width : width + 128], 1, 1)[:, 0:1]
            firsts.append(jnp.where(is_own, own_pos, jnp.where(chosen > 0.5, -1, never)))
        allowed = jnp.where(is_first, firsts[0], firsts[1]) <= query_pos
        scores = dot(keys, pair, 1, 1) * score_scale
        scores = jnp.where(allowed, scores, -1e30)
        top = jnp.max(scores, axis=0, keepdims=True)
        probs = jnp.where(allowed, jnp.exp(scores - top), 0.0)
        total = jnp.sum(probs, axis=0, keepdims=True)
        some = total > 0.0
        scale = jnp.where(some, 1.0 / jnp.where(some, total, 1.0), 0.0)
        latent = dot((probs * scale).astype(bf16), keys, 0, 0).astype(bf16)
        level = jnp.where(some, top + jnp.log(jnp.where(some, total, 1.0)), -1e30)
        terms = three_terms(level)
        at = iota((16, both), 0)
        stats = jnp.zeros((16, both), f32)
        for k, term in enumerate(terms):
            stats = jnp.where(at == k, term, stats)
        stats = stats.astype(bf16)
        for half in range(2):
            head = (own_half ^ half) * n_y + (own_y + n_y - shift) % n_y
            lanes = slice(half * rows, (half + 1) * rows)
            out_ref[head, 0:rows, :] = latent[lanes, :]
            out_ref[head, rows : rows + 16, 0:rows] = stats[:, lanes]
            out_ref[head, rows : rows + 16, rows:] = jnp.zeros((16, keys.shape[1] - rows), bf16)
            gain_ref[head] = ref[half, rows : rows + 16, 0:width]


def project_kernel(rows, part_ref, uv_ref, out_weight_ref, out_ref):
    parts = part_ref.shape[0]
    levels = []
    for s in range(parts):
        stats = part_ref[s, rows : rows + 16, 0:rows].astype(f32)
        levels.append(stats[0:1] + stats[1:2] + stats[2:3])
    top = levels[0]
    for level in levels[1:]:
        top = jnp.maximum(top, level)
    shares = [jnp.exp(level - top) for level in levels]
    total = shares[0]
    for share in shares[1:]:
        total = total + share
    scale = 1.0 / total
    at = iota((rows, rows), 0)
    square = jnp.zeros((rows, rows), f32)
    for s in range(parts):
        square = jnp.where(at == s, shares[s] * scale, square)
    columns = square.T
    latent = columns[:, 0:1] * part_ref[0, 0:rows, :].astype(f32)
    for s in range(1, parts):
        latent = latent + columns[:, s : s + 1] * part_ref[s, 0:rows, :].astype(f32)
    values = dot(latent.astype(bf16), uv_ref[...], 1, 0).astype(bf16)
    width = out_ref.shape[2]
    for d in range(out_ref.shape[0]):
        out_ref[d] = dot(values, out_weight_ref[:, d * width : (d + 1) * width], 1, 0).astype(bf16)


def hidden_kernel(
    part_ref, token_ref, place_ref, router_ref, gain_ref, routes_ref, hidden_ref, rows_ref, pick_ref
):
    attention = part_ref[0].astype(f32)
    for s in range(1, part_ref.shape[0]):
        attention = attention + part_ref[s].astype(f32)
    hidden = (token_ref[...].astype(f32) + attention).astype(bf16)
    hidden_ref[...] = hidden
    rows_ref[...] = dot(place_ref[...], hidden, 1, 0).astype(bf16)
    wide = hidden.astype(f32)
    exact = dict(precision=lax.Precision.HIGHEST)
    scaled = wide * gain_ref[...].astype(f32)
    logits = dot(router_ref[...].astype(f32), scaled, 1, 1, **exact)
    picks = dot(jnp.ones((8, wide.shape[1]), f32), wide * wide, 1, 1, **exact)
    routes = routes_ref[...]
    expert, at = iota(logits.shape, 0), iota(picks.shape, 0)
    for k in range(routes.shape[0]):
        pick = jnp.sum(jnp.where(routes[k : k + 1] == expert, logits, 0.0), axis=0, keepdims=True)
        picks = jnp.where(at == k, pick, picks)
    high, middle, rest = three_terms(picks)
    upper = jnp.concatenate([high, middle], axis=1)
    lower = jnp.concatenate([rest, jnp.zeros_like(rest)], axis=1)
    pick_ref[...] = jnp.concatenate([upper, lower], axis=0).astype(bf16)


def gate_kernel(at_ref, rows_ref, gain_ref, gate_ref, up_ref, gate2_ref, up2_ref, out_ref, normed_ref):
    n_y, _, width = rows_ref.shape
    count, features = normed_ref.shape
    half = at_ref[2]
    squares = jnp.zeros((count, 1), f32)
    for x in range(2):
        for y in range(n_y):
            wide = rows_ref[y, x * count : (x + 1) * count, :].astype(f32)
            squares = squares + jnp.sum(wide * wide, axis=1, keepdims=True)
    inverse = lax.rsqrt(squares / features + epsilon)
    for x in range(2):
        for y in range(n_y):
            s = x * n_y + y
            wide = rows_ref[y, x * count : (x + 1) * count, :].astype(f32)
            scaled = wide * gain_ref[s, 0:1, :].astype(f32)
            normed_ref[:, s * width : (s + 1) * width] = (scaled * inverse).astype(bf16)
    units = gate_ref.shape[0]
    for a, (g_ref, u_ref) in enumerate(((gate_ref, up_ref), (gate2_ref, up2_ref))):
        gate = dot(g_ref[...], normed_ref[...], 1, 1)
        up = dot(u_ref[...], normed_ref[...], 1, 1)
        act = (gate / (1.0 + jnp.exp(-gate)) * up).astype(bf16)
        out_ref[pl.ds(pl.multiple_of((half ^ a) * units, 16), units), :] = act


def down_kernel(at_ref, act_ref, down_ref, down2_ref, out_ref, act_all_ref):
    half = at_ref[2]
    n_y, both, _ = act_ref.shape
    units = both // 2
    for x in range(2):
        for y in range(n_y):
            at = (x * n_y + y) * units
            act_all_ref[at : at + units, :] = act_ref[y, x * units : (x + 1) * units, :]
    for a, ref in enumerate((down_ref, down2_ref)):
        out_ref[half ^ a] = dot(act_all_ref[...], ref[...], 0, 0).astype(bf16)


def combine_kernel(experts, capacity, features, row_ref, routes_ref, place_ref, back_ref, out_ref):
    rows = out_ref.shape[0]
    total = jnp.zeros((8, rows), f32)
    for s in range(row_ref.shape[0]):
        for at in range(experts * capacity, row_ref.shape[1], 16):
            terms = row_ref[s, at : at + 16, :].astype(f32)
            total = total + (terms[0:8, 0:rows] + terms[0:8, rows:] + terms[8:16, 0:rows])
    routes = routes_ref[...]
    top = routes.shape[0]
    inverse = lax.rsqrt(total[top : top + 1] / features + epsilon)
    gates = 1.0 / (1.0 + jnp.exp(-(inverse * total[0:top])))
    gates = gates / jnp.sum(gates, axis=0, keepdims=True)
    expert = iota((experts, rows), 0)
    weight = jnp.zeros((experts, rows), f32)
    for k in range(top):
        weight = jnp.where(routes[k : k + 1] == expert, gates[k : k + 1], weight)
    high = weight.astype(bf16)
    low = (weight - high.astype(f32)).astype(bf16)
    spread = repeat_matrix(experts, capacity)
    place = place_ref[...].astype(f32)
    back = back_ref[...]
    first = dot((dot(spread, high, 1, 0) * place).astype(bf16), back, 0, 0)
    second = dot((dot(spread, low, 1, 0) * place).astype(bf16), back, 0, 0)
    out_ref[...] = (first + second).astype(bf16)


def shape(*dims, dtype=bf16):
    return jax.ShapeDtypeStruct(dims, dtype)


def swap(x, axes):
    return lax.all_to_all(x, axes, split_axis=0, concat_axis=0, tiled=True)


def copies(x, n):
    return jnp.broadcast_to(x[None], (n,) + x.shape)


def all_shifts(x, n):
    turn = lambda k: [(y, (y + k) % n) for y in range(n)]
    return [x] + [lax.ppermute(x, "y", turn(k)) for k in range(1, n)]


def other_half(x):
    return lax.ppermute(x, "xh", [(0, 1), (1, 0)])


CTX, EXP = ("z", "xl"), ("xh", "y")
OWNERS = CTX + ("rep", "xh")


def body(
    queries,
    latents,
    tokens,
    block_mask,
    uv_weight,
    out_weight,
    norm_gain,
    router_matrix,
    routes,
    gate_weight,
    up_weight,
    down_weight,
):
    rows, latent_width = queries.shape[1], queries.shape[3]
    width = tokens.shape[2]
    experts = router_matrix.shape[0]
    capacity = 4 * rows * routes.shape[2] // (3 * experts)
    blocks = block_mask.shape[1]
    n_exp = lax.axis_size(EXP)
    n_y, n_xh = lax.axis_size("y"), lax.axis_size("xh")
    ctx_place, exp_place = lax.axis_index(CTX), lax.axis_index(EXP)
    half = lax.axis_index("xh")
    part_rows = rows // n_exp
    features = width * n_exp
    slots = experts * capacity
    count = slots // n_xh
    units = gate_weight.shape[1]

    own_keys = lax.dynamic_slice_in_dim(latents[0], exp_place * part_rows, part_rows, 0)
    keys = swap(copies(own_keys, blocks), CTX).reshape(blocks * part_rows, latent_width)
    mask_row = lax.dynamic_index_in_dim(block_mask[0], ctx_place, 0, keepdims=True)
    extra = jnp.concatenate(
        [
            norm_gain[None, :],
            mask_row.astype(bf16),
            jnp.zeros((1, latent_width - width - blocks), bf16),
        ],
        axis=1,
    )
    sent = jnp.concatenate(
        [queries[0, :, 0, :], extra, jnp.zeros((15, latent_width), bf16)], axis=0
    )
    other, gate = lax.optimization_barrier((other_half(sent), gate_weight[0]))
    all_queries = all_shifts(jnp.stack([sent, other]), n_y)

    gate2 = other_half(gate)
    up2 = other_half(up_weight[0])
    down2 = other_half(down_weight[0])

    keys, gate2 = lax.optimization_barrier((keys, gate2))

    routes_t = routes[0].T
    place = call(
        lambda *refs: place_kernel(experts, capacity, *refs), shape(slots, rows), routes_t
    )
    at = jnp.stack([ctx_place, exp_place, half, lax.axis_index("y")]).astype(jnp.int32)
    partial, gains = call(
        lambda *refs: attend_kernel(rows, part_rows, *refs),
        [shape(n_exp, rows + 16, latent_width), shape(n_exp, 16, width)],
        at,
        keys,
        *all_queries,
        specs=[in_smem] + [in_vmem] * (1 + n_y),
    )
    partial = swap(partial, EXP)
    terms = call(
        lambda *refs: project_kernel(rows, *refs),
        shape(n_exp, rows, width),
        partial,
        uv_weight[0],
        out_weight[0],
    )
    terms = swap(terms, EXP)
    hidden, picked, picks = call(
        hidden_kernel,
        [shape(rows, width), shape(slots, width), shape(16, width)],
        terms,
        tokens[0],
        place,
        router_matrix,
        norm_gain[None, :],
        routes_t,
    )
    received = swap(picked.reshape(experts * n_xh, capacity // n_xh, width), OWNERS)
    received, up2 = lax.optimization_barrier((received, up2))
    received = received.reshape(experts, n_xh, capacity // n_xh, width).swapaxes(0, 1)
    mine = jnp.concatenate([received.reshape(slots, width), picks, other_half(picks)], axis=0)
    full_rows, down2 = lax.optimization_barrier((swap(copies(mine, n_y), "y"), down2))
    act = call(
        gate_kernel,
        shape(n_xh * units, count),
        at,
        full_rows,
        gains,
        gate_weight[0],
        up_weight[0],
        gate2,
        up2,
        specs=[in_smem] + [in_vmem] * 6,
        scratch=[pltpu.VMEM((count, features), bf16)],
    )
    act = swap(copies(act, n_y), "y")
    out = call(
        down_kernel,
        shape(n_xh, count, width),
        at,
        act,
        down_weight[0],
        down2,
        specs=[in_smem] + [in_vmem] * 3,
        scratch=[pltpu.VMEM((n_exp * units, count), bf16)],
    )
    out = out.reshape(n_xh, experts, capacity // n_xh, width).swapaxes(0, 1)
    back = swap(out.reshape(experts * n_xh, capacity // n_xh, width), OWNERS)
    back = back.reshape(slots, width)
    routed = call(
        lambda *refs: combine_kernel(experts, capacity, features, *refs),
        shape(rows, width),
        full_rows,
        routes_t,
        place,
        back,
    )
    return (hidden[None], routed[None])


def solution(mesh):
    sizes = mesh.shape
    fine = Mesh(
        mesh.devices.reshape(sizes["ctx"] // 2, 2, 2, sizes["exp"] // 2, sizes["rep"]),
        ("z", "xl", "xh", "y", "rep"),
    )
    placed = (
        P("rep", CTX, EXP, None),
        P("rep", CTX, None),
        P("rep", CTX, EXP),
        P(EXP, None, None),
        P(EXP, None, None),
        P(EXP, None, None),
        P(EXP),
        P(None, EXP),
        P("rep", CTX, None),
        P(CTX + ("rep",), EXP, None),
        P(CTX + ("rep",), EXP, None),
        P(CTX + ("rep",), None, EXP),
    )
    return jax.shard_map(
        body,
        mesh=fine,
        in_specs=placed,
        out_specs=(P("rep", CTX, EXP), P("rep", CTX, EXP)),
        check_vma=False,
    )
```

```python
import jax
import jax.numpy as jnp
from jax import lax
from jax.experimental import pallas as pl
from jax.experimental.pallas import tpu as pltpu
from jax.sharding import Mesh, PartitionSpec as P

score_scale = 192.0 ** (-0.5)
epsilon = 1e-06
never = 1 << 20

f32 = jnp.float32
bf16 = jnp.bfloat16

in_vmem = pl.BlockSpec(memory_space=pltpu.VMEM)
in_smem = pl.BlockSpec(memory_space=pltpu.SMEM)


def iota(shape, dim):
    return lax.broadcasted_iota(jnp.int32, shape, dim)


def dot(a, b, ca, cb, **kw):
    return lax.dot_general(a, b, (((ca,), (cb,)), ((), ())), preferred_element_type=f32, **kw)


def call(kernel, outs, *operands, specs=None, scratch=(), limit=24):
    many = isinstance(outs, list)
    return pl.pallas_call(
        kernel,
        out_shape=outs,
        in_specs=specs or [in_vmem] * len(operands),
        out_specs=[in_vmem] * len(outs) if many else in_vmem,
        scratch_shapes=list(scratch),
        compiler_params=pltpu.CompilerParams(vmem_limit_bytes=limit << 20),
    )(*operands)


def three_terms(x):
    high = x.astype(bf16).astype(f32)
    middle = (x - high).astype(bf16).astype(f32)
    return high, middle, x - high - middle


def repeat_matrix(experts, capacity):
    tall = (experts * capacity, experts)
    return (iota(tall, 0) // capacity == iota(tall, 1)).astype(f32).astype(bf16)


def place_kernel(experts, capacity, routes_ref, place_ref):
    top, rows = routes_ref.shape
    routes = routes_ref[...]
    expert = iota((experts, rows), 0)
    member = routes[0:1] == expert
    for k in range(1, top):
        member = member | (routes[k : k + 1] == expert)
    earlier = (iota((rows, rows), 0) < iota((rows, rows), 1)).astype(f32).astype(bf16)
    count = dot(member.astype(f32).astype(bf16), earlier, 1, 0)
    code = jnp.where(member, count, -1.0).astype(bf16)
    spread = dot(repeat_matrix(experts, capacity), code, 1, 0)
    slot = iota((experts * capacity, rows), 0) % capacity
    place_ref[...] = (spread == slot.astype(f32)).astype(f32).astype(bf16)


def attend_kernel(rows, part_rows, at_ref, key_ref, *refs):
    pair_refs, out_ref, gain_ref = refs[:-2], refs[-2], refs[-1]
    own_block, own_part, own_half, own_y = at_ref[0], at_ref[1], at_ref[2], at_ref[3]
    n_y = len(pair_refs)
    keys = key_ref[...]
    count = keys.shape[0]
    lane = iota((count, 128), 1)
    block = iota((count, 128), 0) // part_rows
    earlier = ((block == lane) & (lane < own_block)).astype(f32).astype(bf16)
    key_row = iota((count, 1), 0)
    is_own = key_row // part_rows == own_block
    own_pos = own_part * part_rows + key_row % part_rows
    both = 2 * rows
    is_first = iota((1, both), 1) < rows
    query_pos = iota((count, both), 1) % rows
    width = gain_ref.shape[2]
    for shift in range(n_y):
        ref = pair_refs[shift]
        pair = jnp.concatenate([ref[0, 0:rows, :], ref[1, 0:rows, :]], axis=0)
        firsts = []
        for half in range(2):
            chosen = dot(earlier, ref[half, rows : rows + 16, width : width + 128], 1, 1)[:, 0:1]
            firsts.append(jnp.where(is_own, own_pos, jnp.where(chosen > 0.5, -1, never)))
        allowed = jnp.where(is_first, firsts[0], firsts[1]) <= query_pos
        scores = dot(keys, pair, 1, 1) * score_scale
        scores = jnp.where(allowed, scores, -1e30)
        top = jnp.max(scores, axis=0, keepdims=True)
        probs = jnp.where(allowed, jnp.exp(scores - top), 0.0)
        total = jnp.sum(probs, axis=0, keepdims=True)
        some = total > 0.0
        scale = jnp.where(some, 1.0 / jnp.where(some, total, 1.0), 0.0)
        latent = dot((probs * scale).astype(bf16), keys, 0, 0).astype(bf16)
        level = jnp.where(some, top + jnp.log(jnp.where(some, total, 1.0)), -1e30)
        terms = three_terms(level)
        at = iota((16, both), 0)
        stats = jnp.zeros((16, both), f32)
        for k, term in enumerate(terms):
            stats = jnp.where(at == k, term, stats)
        stats = stats.astype(bf16)
        for half in range(2):
            head = (own_half ^ half) * n_y + (own_y + n_y - shift) % n_y
            lanes = slice(half * rows, (half + 1) * rows)
            out_ref[head, 0:rows, :] = latent[lanes, :]
            out_ref[head, rows : rows + 16, 0:rows] = stats[:, lanes]
            out_ref[head, rows : rows + 16, rows:] = jnp.zeros((16, keys.shape[1] - rows), bf16)
            gain_ref[head] = ref[half, rows : rows + 16, 0:width]


def project_kernel(rows, part_ref, uv_ref, out_weight_ref, out_ref):
    parts = part_ref.shape[0]
    levels = []
    for s in range(parts):
        stats = part_ref[s, rows : rows + 16, 0:rows].astype(f32)
        levels.append(stats[0:1] + stats[1:2] + stats[2:3])
    top = levels[0]
    for level in levels[1:]:
        top = jnp.maximum(top, level)
    shares = [jnp.exp(level - top) for level in levels]
    total = shares[0]
    for share in shares[1:]:
        total = total + share
    scale = 1.0 / total
    at = iota((rows, rows), 0)
    square = jnp.zeros((rows, rows), f32)
    for s in range(parts):
        square = jnp.where(at == s, shares[s] * scale, square)
    columns = square.T
    latent = columns[:, 0:1] * part_ref[0, 0:rows, :].astype(f32)
    for s in range(1, parts):
        latent = latent + columns[:, s : s + 1] * part_ref[s, 0:rows, :].astype(f32)
    values = dot(latent.astype(bf16), uv_ref[...], 1, 0).astype(bf16)
    width = out_ref.shape[2]
    for d in range(out_ref.shape[0]):
        out_ref[d] = dot(values, out_weight_ref[:, d * width : (d + 1) * width], 1, 0).astype(bf16)


def hidden_kernel(
    part_ref, token_ref, place_ref, router_ref, gain_ref, routes_ref, hidden_ref, rows_ref, pick_ref
):
    attention = part_ref[0].astype(f32)
    for s in range(1, part_ref.shape[0]):
        attention = attention + part_ref[s].astype(f32)
    hidden = (token_ref[...].astype(f32) + attention).astype(bf16)
    hidden_ref[...] = hidden
    rows_ref[...] = dot(place_ref[...], hidden, 1, 0).astype(bf16)
    wide = hidden.astype(f32)
    exact = dict(precision=lax.Precision.HIGHEST)
    scaled = wide * gain_ref[...].astype(f32)
    logits = dot(router_ref[...].astype(f32), scaled, 1, 1, **exact)
    picks = dot(jnp.ones((8, wide.shape[1]), f32), wide * wide, 1, 1, **exact)
    routes = routes_ref[...]
    expert, at = iota(logits.shape, 0), iota(picks.shape, 0)
    for k in range(routes.shape[0]):
        pick = jnp.sum(jnp.where(routes[k : k + 1] == expert, logits, 0.0), axis=0, keepdims=True)
        picks = jnp.where(at == k, pick, picks)
    high, middle, rest = three_terms(picks)
    upper = jnp.concatenate([high, middle], axis=1)
    lower = jnp.concatenate([rest, jnp.zeros_like(rest)], axis=1)
    pick_ref[...] = jnp.concatenate([upper, lower], axis=0).astype(bf16)


def gate_kernel(
    at_ref, own_ref, low_ref, high_ref, far0_ref, far1_ref, gain_ref,
    gate_ref, up_ref, gate2_ref, up2_ref, out_ref, normed_ref,
):
    count, features = normed_ref.shape
    width = own_ref.shape[1]
    half, own_y = at_ref[2], at_ref[3]
    n_y = features // width // 2
    pieces = []
    for shift, first, second in (
        (0, own_ref, own_ref),
        (n_y - 1, low_ref, low_ref),
        (1, high_ref, high_ref),
        (2, far0_ref, far1_ref),
    ):
        y = (own_y + shift) % n_y
        pieces.append((y, first, 0))
        pieces.append((n_y + y, second, second.shape[0] - 32 - count))
    squares = jnp.zeros((count, 1), f32)
    for _, ref, at in pieces:
        wide = ref[at : at + count, :].astype(f32)
        squares = squares + jnp.sum(wide * wide, axis=1, keepdims=True)
    inverse = lax.rsqrt(squares / features + epsilon)
    for s, ref, at in pieces:
        scaled = ref[at : at + count, :].astype(f32) * gain_ref[s][0:1].astype(f32)
        lanes = pl.ds(pl.multiple_of(s * width, 128), width)
        normed_ref[:, lanes] = (scaled * inverse).astype(bf16)
    units = gate_ref.shape[0]
    for a, (g_ref, u_ref) in enumerate(((gate_ref, up_ref), (gate2_ref, up2_ref))):
        gate = dot(g_ref[...], normed_ref[...], 1, 1)
        up = dot(u_ref[...], normed_ref[...], 1, 1)
        act = (gate / (1.0 + jnp.exp(-gate)) * up).astype(bf16)
        out_ref[pl.ds(pl.multiple_of((half ^ a) * units, 16), units), :] = act


def down_kernel(at_ref, act_ref, down_ref, down2_ref, out_ref, act_all_ref):
    half = at_ref[2]
    n_y, both, _ = act_ref.shape
    units = both // 2
    for x in range(2):
        for y in range(n_y):
            at = (x * n_y + y) * units
            act_all_ref[at : at + units, :] = act_ref[y, x * units : (x + 1) * units, :]
    for a, ref in enumerate((down_ref, down2_ref)):
        out_ref[half ^ a] = dot(act_all_ref[...], ref[...], 0, 0).astype(bf16)


def combine_kernel(experts, capacity, features, routes_ref, place_ref, back_ref, *refs):
    row_refs, out_ref = refs[:-1], refs[-1]
    rows = out_ref.shape[0]
    total = jnp.zeros((8, rows), f32)
    for ref in row_refs:
        for at in range(ref.shape[0] - 32, ref.shape[0], 16):
            terms = ref[at : at + 16, :].astype(f32)
            total = total + (terms[0:8, 0:rows] + terms[0:8, rows:] + terms[8:16, 0:rows])
    routes = routes_ref[...]
    top = routes.shape[0]
    inverse = lax.rsqrt(total[top : top + 1] / features + epsilon)
    gates = 1.0 / (1.0 + jnp.exp(-(inverse * total[0:top])))
    gates = gates / jnp.sum(gates, axis=0, keepdims=True)
    expert = iota((experts, rows), 0)
    weight = jnp.zeros((experts, rows), f32)
    for k in range(top):
        weight = jnp.where(routes[k : k + 1] == expert, gates[k : k + 1], weight)
    high = weight.astype(bf16)
    low = (weight - high.astype(f32)).astype(bf16)
    spread = repeat_matrix(experts, capacity)
    place = place_ref[...].astype(f32)
    back = back_ref[...]
    first = dot((dot(spread, high, 1, 0) * place).astype(bf16), back, 0, 0)
    second = dot((dot(spread, low, 1, 0) * place).astype(bf16), back, 0, 0)
    out_ref[...] = (first + second).astype(bf16)


def shape(*dims, dtype=bf16):
    return jax.ShapeDtypeStruct(dims, dtype)


def swap(x, axes):
    return lax.all_to_all(x, axes, split_axis=0, concat_axis=0, tiled=True)


def copies(x, n):
    return jnp.broadcast_to(x[None], (n,) + x.shape)


def all_shifts(x, n):
    turn = lambda k: [(y, (y + k) % n) for y in range(n)]
    return [x] + [lax.ppermute(x, "y", turn(k)) for k in range(1, n)]


def other_half(x):
    return lax.ppermute(x, "xh", [(0, 1), (1, 0)])


CTX, EXP = ("z", "xl"), ("xh", "y")
OWNERS = CTX + ("rep", "xh")


def body(
    queries,
    latents,
    tokens,
    block_mask,
    uv_weight,
    out_weight,
    norm_gain,
    router_matrix,
    routes,
    gate_weight,
    up_weight,
    down_weight,
):
    rows, latent_width = queries.shape[1], queries.shape[3]
    width = tokens.shape[2]
    experts = router_matrix.shape[0]
    capacity = 4 * rows * routes.shape[2] // (3 * experts)
    blocks = block_mask.shape[1]
    n_exp = lax.axis_size(EXP)
    n_y, n_xh = lax.axis_size("y"), lax.axis_size("xh")
    ctx_place, exp_place = lax.axis_index(CTX), lax.axis_index(EXP)
    half = lax.axis_index("xh")
    part_rows = rows // n_exp
    features = width * n_exp
    slots = experts * capacity
    count = slots // n_xh
    units = gate_weight.shape[1]

    own_keys = lax.dynamic_slice_in_dim(latents[0], exp_place * part_rows, part_rows, 0)
    keys = swap(copies(own_keys, blocks), CTX).reshape(blocks * part_rows, latent_width)
    mask_row = lax.dynamic_index_in_dim(block_mask[0], ctx_place, 0, keepdims=True)
    extra = jnp.concatenate(
        [
            norm_gain[None, :],
            mask_row.astype(bf16),
            jnp.zeros((1, latent_width - width - blocks), bf16),
        ],
        axis=1,
    )
    sent = jnp.concatenate(
        [queries[0, :, 0, :], extra, jnp.zeros((15, latent_width), bf16)], axis=0
    )
    other, gate = lax.optimization_barrier((other_half(sent), gate_weight[0]))
    all_queries = all_shifts(jnp.stack([sent, other]), n_y)

    gate2 = other_half(gate)
    up2 = other_half(up_weight[0])
    down2 = other_half(down_weight[0])

    keys, gate2 = lax.optimization_barrier((keys, gate2))

    routes_t = routes[0].T
    place = call(
        lambda *refs: place_kernel(experts, capacity, *refs), shape(slots, rows), routes_t
    )
    at = jnp.stack([ctx_place, exp_place, half, lax.axis_index("y")]).astype(jnp.int32)
    partial, gains = call(
        lambda *refs: attend_kernel(rows, part_rows, *refs),
        [shape(n_exp, rows + 16, latent_width), shape(n_exp, 16, width)],
        at,
        keys,
        *all_queries,
        specs=[in_smem] + [in_vmem] * (1 + n_y),
    )
    partial = swap(partial, EXP)
    terms = call(
        lambda *refs: project_kernel(rows, *refs),
        shape(n_exp, rows, width),
        partial,
        uv_weight[0],
        out_weight[0],
    )
    terms = swap(terms, EXP)
    hidden, picked, picks = call(
        hidden_kernel,
        [shape(rows, width), shape(slots, width), shape(16, width)],
        terms,
        tokens[0],
        place,
        router_matrix,
        norm_gain[None, :],
        routes_t,
    )
    received = swap(picked.reshape(experts * n_xh, capacity // n_xh, width), OWNERS)
    received, up2 = lax.optimization_barrier((received, up2))
    received = received.reshape(experts, n_xh, capacity // n_xh, width).swapaxes(0, 1)
    mine = jnp.concatenate([received.reshape(slots, width), picks, other_half(picks)], axis=0)
    up_turn = [(y, (y + 1) % n_y) for y in range(n_y)]
    down_turn = [(y, (y + n_y - 1) % n_y) for y in range(n_y)]
    low = lax.ppermute(mine, "y", up_turn)
    high = lax.ppermute(mine, "y", down_turn)
    far0 = lax.ppermute(low[0:count], "y", up_turn)
    far1 = lax.ppermute(high[count:], "y", down_turn)
    far0, far1, down2 = lax.optimization_barrier((far0, far1, down2))
    act = call(
        gate_kernel,
        shape(n_xh * units, count),
        at,
        mine,
        low,
        high,
        far0,
        far1,
        gains,
        gate_weight[0],
        up_weight[0],
        gate2,
        up2,
        specs=[in_smem] + [in_vmem] * 10,
        scratch=[pltpu.VMEM((count, features), bf16)],
    )
    act = swap(copies(act, n_y), "y")
    out = call(
        down_kernel,
        shape(n_xh, count, width),
        at,
        act,
        down_weight[0],
        down2,
        specs=[in_smem] + [in_vmem] * 3,
        scratch=[pltpu.VMEM((n_exp * units, count), bf16)],
    )
    out = out.reshape(n_xh, experts, capacity // n_xh, width).swapaxes(0, 1)
    back = swap(out.reshape(experts * n_xh, capacity // n_xh, width), OWNERS)
    back = back.reshape(slots, width)
    routed = call(
        lambda *refs: combine_kernel(experts, capacity, features, *refs),
        shape(rows, width),
        routes_t,
        place,
        back,
        mine,
        low,
        high,
        far1,
    )
    return (hidden[None], routed[None])


def solution(mesh):
    sizes = mesh.shape
    fine = Mesh(
        mesh.devices.reshape(sizes["ctx"] // 2, 2, 2, sizes["exp"] // 2, sizes["rep"]),
        ("z", "xl", "xh", "y", "rep"),
    )
    placed = (
        P("rep", CTX, EXP, None),
        P("rep", CTX, None),
        P("rep", CTX, EXP),
        P(EXP, None, None),
        P(EXP, None, None),
        P(EXP, None, None),
        P(EXP),
        P(None, EXP),
        P("rep", CTX, None),
        P(CTX + ("rep",), EXP, None),
        P(CTX + ("rep",), EXP, None),
        P(CTX + ("rep",), None, EXP),
    )
    return jax.shard_map(
        body,
        mesh=fine,
        in_specs=placed,
        out_specs=(P("rep", CTX, EXP), P("rep", CTX, EXP)),
        check_vma=False,
    )
```

```python
import jax
import jax.numpy as jnp
from jax import lax
from jax.experimental import pallas as pl
from jax.experimental.pallas import tpu as pltpu
from jax.sharding import Mesh, PartitionSpec as P

score_scale = 192.0 ** (-0.5)
epsilon = 1e-06
never = 1 << 20

f32 = jnp.float32
bf16 = jnp.bfloat16

in_vmem = pl.BlockSpec(memory_space=pltpu.VMEM)
in_smem = pl.BlockSpec(memory_space=pltpu.SMEM)


def iota(shape, dim):
    return lax.broadcasted_iota(jnp.int32, shape, dim)


def dot(a, b, ca, cb, **kw):
    return lax.dot_general(a, b, (((ca,), (cb,)), ((), ())), preferred_element_type=f32, **kw)


def call(kernel, outs, *operands, specs=None, scratch=(), limit=24):
    many = isinstance(outs, list)
    return pl.pallas_call(
        kernel,
        out_shape=outs,
        in_specs=specs or [in_vmem] * len(operands),
        out_specs=[in_vmem] * len(outs) if many else in_vmem,
        scratch_shapes=list(scratch),
        compiler_params=pltpu.CompilerParams(vmem_limit_bytes=limit << 20),
    )(*operands)


def three_terms(x):
    high = x.astype(bf16).astype(f32)
    middle = (x - high).astype(bf16).astype(f32)
    return high, middle, x - high - middle


def repeat_matrix(experts, capacity):
    tall = (experts * capacity, experts)
    return (iota(tall, 0) // capacity == iota(tall, 1)).astype(f32).astype(bf16)


def place_kernel(experts, capacity, routes_ref, place_ref):
    top, rows = routes_ref.shape
    routes = routes_ref[...]
    expert = iota((experts, rows), 0)
    member = routes[0:1] == expert
    for k in range(1, top):
        member = member | (routes[k : k + 1] == expert)
    earlier = (iota((rows, rows), 0) < iota((rows, rows), 1)).astype(f32).astype(bf16)
    count = dot(member.astype(f32).astype(bf16), earlier, 1, 0)
    code = jnp.where(member, count, -1.0).astype(bf16)
    spread = dot(repeat_matrix(experts, capacity), code, 1, 0)
    slot = iota((experts * capacity, rows), 0) % capacity
    place_ref[...] = (spread == slot.astype(f32)).astype(f32).astype(bf16)


def attend_kernel(rows, part_rows, at_ref, key_ref, *refs):
    pair_refs, out_ref, gain_ref = refs[:-2], refs[-2], refs[-1]
    own_block, own_part, own_half, own_y = at_ref[0], at_ref[1], at_ref[2], at_ref[3]
    n_y = len(pair_refs)
    keys = key_ref[...]
    count = keys.shape[0]
    lane = iota((count, 128), 1)
    block = iota((count, 128), 0) // part_rows
    earlier = ((block == lane) & (lane < own_block)).astype(f32).astype(bf16)
    key_row = iota((count, 1), 0)
    is_own = key_row // part_rows == own_block
    own_pos = own_part * part_rows + key_row % part_rows
    both = 2 * rows
    is_first = iota((1, both), 1) < rows
    query_pos = iota((count, both), 1) % rows
    width = gain_ref.shape[2]
    for shift in range(n_y):
        ref = pair_refs[shift]
        pair = jnp.concatenate([ref[0, 0:rows, :], ref[1, 0:rows, :]], axis=0)
        firsts = []
        for half in range(2):
            chosen = dot(earlier, ref[half, rows : rows + 16, width : width + 128], 1, 1)[:, 0:1]
            firsts.append(jnp.where(is_own, own_pos, jnp.where(chosen > 0.5, -1, never)))
        allowed = jnp.where(is_first, firsts[0], firsts[1]) <= query_pos
        scores = dot(keys, pair, 1, 1) * score_scale
        scores = jnp.where(allowed, scores, -1e30)
        top = jnp.max(scores, axis=0, keepdims=True)
        probs = jnp.where(allowed, jnp.exp(scores - top), 0.0)
        total = jnp.sum(probs, axis=0, keepdims=True)
        some = total > 0.0
        scale = jnp.where(some, 1.0 / jnp.where(some, total, 1.0), 0.0)
        latent = dot((probs * scale).astype(bf16), keys, 0, 0).astype(bf16)
        level = jnp.where(some, top + jnp.log(jnp.where(some, total, 1.0)), -1e30)
        terms = three_terms(level)
        at = iota((16, both), 0)
        stats = jnp.zeros((16, both), f32)
        for k, term in enumerate(terms):
            stats = jnp.where(at == k, term, stats)
        stats = stats.astype(bf16)
        for half in range(2):
            head = (own_half ^ half) * n_y + (own_y + n_y - shift) % n_y
            lanes = slice(half * rows, (half + 1) * rows)
            out_ref[head, 0:rows, :] = latent[lanes, :]
            out_ref[head, rows : rows + 16, 0:rows] = stats[:, lanes]
            out_ref[head, rows : rows + 16, rows:] = jnp.zeros((16, keys.shape[1] - rows), bf16)
            gain_ref[head] = ref[half, rows : rows + 16, 0:width]


def project_kernel(rows, part_ref, uv_ref, out_weight_ref, out_ref):
    parts = part_ref.shape[0]
    levels = []
    for s in range(parts):
        stats = part_ref[s, rows : rows + 16, 0:rows].astype(f32)
        levels.append(stats[0:1] + stats[1:2] + stats[2:3])
    top = levels[0]
    for level in levels[1:]:
        top = jnp.maximum(top, level)
    shares = [jnp.exp(level - top) for level in levels]
    total = shares[0]
    for share in shares[1:]:
        total = total + share
    scale = 1.0 / total
    at = iota((rows, rows), 0)
    square = jnp.zeros((rows, rows), f32)
    for s in range(parts):
        square = jnp.where(at == s, shares[s] * scale, square)
    columns = square.T
    latent = columns[:, 0:1] * part_ref[0, 0:rows, :].astype(f32)
    for s in range(1, parts):
        latent = latent + columns[:, s : s + 1] * part_ref[s, 0:rows, :].astype(f32)
    values = dot(latent.astype(bf16), uv_ref[...], 1, 0).astype(bf16)
    width = out_ref.shape[2]
    for d in range(out_ref.shape[0]):
        out_ref[d] = dot(values, out_weight_ref[:, d * width : (d + 1) * width], 1, 0).astype(bf16)


def hidden_kernel(
    part_ref, token_ref, place_ref, router_ref, gain_ref, routes_ref, hidden_ref, rows_ref, pick_ref
):
    attention = part_ref[0].astype(f32)
    for s in range(1, part_ref.shape[0]):
        attention = attention + part_ref[s].astype(f32)
    hidden = (token_ref[...].astype(f32) + attention).astype(bf16)
    hidden_ref[...] = hidden
    rows_ref[...] = dot(place_ref[...], hidden, 1, 0).astype(bf16)
    wide = hidden.astype(f32)
    exact = dict(precision=lax.Precision.HIGHEST)
    scaled = wide * gain_ref[...].astype(f32)
    logits = dot(router_ref[...].astype(f32), scaled, 1, 1, **exact)
    picks = dot(jnp.ones((8, wide.shape[1]), f32), wide * wide, 1, 1, **exact)
    routes = routes_ref[...]
    expert, at = iota(logits.shape, 0), iota(picks.shape, 0)
    for k in range(routes.shape[0]):
        pick = jnp.sum(jnp.where(routes[k : k + 1] == expert, logits, 0.0), axis=0, keepdims=True)
        picks = jnp.where(at == k, pick, picks)
    high, middle, rest = three_terms(picks)
    upper = jnp.concatenate([high, middle], axis=1)
    lower = jnp.concatenate([rest, jnp.zeros_like(rest)], axis=1)
    pick_ref[...] = jnp.concatenate([upper, lower], axis=0).astype(bf16)


def gate_kernel(
    at_ref, own_ref, low_ref, high_ref, far0_ref, far1_ref, gain_ref,
    gate_ref, up_ref, gate2_ref, up2_ref, out_ref, normed_ref,
):
    count, features = normed_ref.shape
    width = own_ref.shape[1]
    half, own_y = at_ref[2], at_ref[3]
    n_y = features // width // 2
    pieces = []
    for shift, first, second in (
        (0, own_ref, own_ref),
        (n_y - 1, low_ref, low_ref),
        (1, high_ref, high_ref),
        (2, far0_ref, far1_ref),
    ):
        y = (own_y + shift) % n_y
        pieces.append((y, first, 0))
        pieces.append((n_y + y, second, second.shape[0] - 32 - count))
    squares = jnp.zeros((count, 1), f32)
    for _, ref, at in pieces:
        wide = ref[at : at + count, :].astype(f32)
        squares = squares + jnp.sum(wide * wide, axis=1, keepdims=True)
    inverse = lax.rsqrt(squares / features + epsilon)
    for s, ref, at in pieces:
        scaled = ref[at : at + count, :].astype(f32) * gain_ref[s][0:1].astype(f32)
        lanes = pl.ds(pl.multiple_of(s * width, 128), width)
        normed_ref[:, lanes] = (scaled * inverse).astype(bf16)
    units = gate_ref.shape[0]
    for a, (g_ref, u_ref) in enumerate(((gate_ref, up_ref), (gate2_ref, up2_ref))):
        gate = dot(g_ref[...], normed_ref[...], 1, 1)
        up = dot(u_ref[...], normed_ref[...], 1, 1)
        act = (gate / (1.0 + jnp.exp(-gate)) * up).astype(bf16)
        out_ref[pl.ds(pl.multiple_of((half ^ a) * units, 16), units), :] = act


def down_kernel(at_ref, act_ref, down_ref, down2_ref, out_ref, act_all_ref):
    half = at_ref[2]
    n_y, both, _ = act_ref.shape
    units = both // 2
    for x in range(2):
        for y in range(n_y):
            at = (x * n_y + y) * units
            act_all_ref[at : at + units, :] = act_ref[y, x * units : (x + 1) * units, :]
    for a, ref in enumerate((down_ref, down2_ref)):
        out_ref[half ^ a] = dot(act_all_ref[...], ref[...], 0, 0).astype(bf16)


def combine_kernel(experts, capacity, features, routes_ref, place_ref, back_ref, *refs):
    row_refs, out_ref = refs[:-1], refs[-1]
    rows = out_ref.shape[0]
    total = jnp.zeros((8, rows), f32)
    for ref in row_refs:
        for at in range(ref.shape[0] - 32, ref.shape[0], 16):
            terms = ref[at : at + 16, :].astype(f32)
            total = total + (terms[0:8, 0:rows] + terms[0:8, rows:] + terms[8:16, 0:rows])
    routes = routes_ref[...]
    top = routes.shape[0]
    inverse = lax.rsqrt(total[top : top + 1] / features + epsilon)
    gates = 1.0 / (1.0 + jnp.exp(-(inverse * total[0:top])))
    gates = gates / jnp.sum(gates, axis=0, keepdims=True)
    expert = iota((experts, rows), 0)
    weight = jnp.zeros((experts, rows), f32)
    for k in range(top):
        weight = jnp.where(routes[k : k + 1] == expert, gates[k : k + 1], weight)
    high = weight.astype(bf16)
    low = (weight - high.astype(f32)).astype(bf16)
    spread = repeat_matrix(experts, capacity)
    place = place_ref[...].astype(f32)
    back = back_ref[...]
    first = dot((dot(spread, high, 1, 0) * place).astype(bf16), back, 0, 0)
    second = dot((dot(spread, low, 1, 0) * place).astype(bf16), back, 0, 0)
    out_ref[...] = (first + second).astype(bf16)


def shape(*dims, dtype=bf16):
    return jax.ShapeDtypeStruct(dims, dtype)


def swap(x, axes):
    return lax.all_to_all(x, axes, split_axis=0, concat_axis=0, tiled=True)


def copies(x, n):
    return jnp.broadcast_to(x[None], (n,) + x.shape)


def all_shifts(x, n):
    turn = lambda k: [(y, (y + k) % n) for y in range(n)]
    return [x] + [lax.ppermute(x, "y", turn(k)) for k in range(1, n)]


def other_half(x):
    return lax.ppermute(x, "xh", [(0, 1), (1, 0)])


CTX, EXP = ("z", "xl"), ("xh", "y")
OWNERS = CTX + ("rep", "xh")


def body(
    queries,
    latents,
    tokens,
    block_mask,
    uv_weight,
    out_weight,
    norm_gain,
    router_matrix,
    routes,
    gate_weight,
    up_weight,
    down_weight,
):
    rows, latent_width = queries.shape[1], queries.shape[3]
    width = tokens.shape[2]
    experts = router_matrix.shape[0]
    capacity = 4 * rows * routes.shape[2] // (3 * experts)
    blocks = block_mask.shape[1]
    n_exp = lax.axis_size(EXP)
    n_y, n_xh = lax.axis_size("y"), lax.axis_size("xh")
    ctx_place, exp_place = lax.axis_index(CTX), lax.axis_index(EXP)
    half = lax.axis_index("xh")
    part_rows = rows // n_exp
    features = width * n_exp
    slots = experts * capacity
    count = slots // n_xh
    units = gate_weight.shape[1]

    own_keys = lax.dynamic_slice_in_dim(latents[0], exp_place * part_rows, part_rows, 0)
    keys = swap(copies(own_keys, blocks), CTX).reshape(blocks * part_rows, latent_width)
    mask_row = lax.dynamic_index_in_dim(block_mask[0], ctx_place, 0, keepdims=True)
    extra = jnp.concatenate(
        [
            norm_gain[None, :],
            mask_row.astype(bf16),
            jnp.zeros((1, latent_width - width - blocks), bf16),
        ],
        axis=1,
    )
    sent = jnp.concatenate(
        [queries[0, :, 0, :], extra, jnp.zeros((15, latent_width), bf16)], axis=0
    )
    other, gate = lax.optimization_barrier((other_half(sent), gate_weight[0]))
    all_queries = all_shifts(jnp.stack([sent, other]), n_y)

    gate2 = other_half(gate)
    up2 = other_half(up_weight[0])
    down2 = other_half(down_weight[0])


    routes_t = routes[0].T
    place = call(
        lambda *refs: place_kernel(experts, capacity, *refs), shape(slots, rows), routes_t
    )
    at = jnp.stack([ctx_place, exp_place, half, lax.axis_index("y")]).astype(jnp.int32)
    partial, gains = call(
        lambda *refs: attend_kernel(rows, part_rows, *refs),
        [shape(n_exp, rows + 16, latent_width), shape(n_exp, 16, width)],
        at,
        keys,
        *all_queries,
        specs=[in_smem] + [in_vmem] * (1 + n_y),
    )
    partial, gate2 = lax.optimization_barrier((partial, gate2))
    partial = swap(partial, EXP)
    terms = call(
        lambda *refs: project_kernel(rows, *refs),
        shape(n_exp, rows, width),
        partial,
        uv_weight[0],
        out_weight[0],
    )
    terms = swap(terms, EXP)
    hidden, picked, picks = call(
        hidden_kernel,
        [shape(rows, width), shape(slots, width), shape(16, width)],
        terms,
        tokens[0],
        place,
        router_matrix,
        norm_gain[None, :],
        routes_t,
    )
    received = swap(picked.reshape(experts * n_xh, capacity // n_xh, width), OWNERS)
    received, up2 = lax.optimization_barrier((received, up2))
    received = received.reshape(experts, n_xh, capacity // n_xh, width).swapaxes(0, 1)
    mine = jnp.concatenate([received.reshape(slots, width), picks, other_half(picks)], axis=0)
    up_turn = [(y, (y + 1) % n_y) for y in range(n_y)]
    down_turn = [(y, (y + n_y - 1) % n_y) for y in range(n_y)]
    low = lax.ppermute(mine, "y", up_turn)
    high = lax.ppermute(mine, "y", down_turn)
    far0 = lax.ppermute(low[0:count], "y", up_turn)
    far1 = lax.ppermute(high[count:], "y", down_turn)
    far0, far1, down2 = lax.optimization_barrier((far0, far1, down2))
    act = call(
        gate_kernel,
        shape(n_xh * units, count),
        at,
        mine,
        low,
        high,
        far0,
        far1,
        gains,
        gate_weight[0],
        up_weight[0],
        gate2,
        up2,
        specs=[in_smem] + [in_vmem] * 10,
        scratch=[pltpu.VMEM((count, features), bf16)],
    )
    act = swap(copies(act, n_y), "y")
    out = call(
        down_kernel,
        shape(n_xh, count, width),
        at,
        act,
        down_weight[0],
        down2,
        specs=[in_smem] + [in_vmem] * 3,
        scratch=[pltpu.VMEM((n_exp * units, count), bf16)],
    )
    out = out.reshape(n_xh, experts, capacity // n_xh, width).swapaxes(0, 1)
    back = swap(out.reshape(experts * n_xh, capacity // n_xh, width), OWNERS)
    back = back.reshape(slots, width)
    routed = call(
        lambda *refs: combine_kernel(experts, capacity, features, *refs),
        shape(rows, width),
        routes_t,
        place,
        back,
        mine,
        low,
        high,
        far1,
    )
    return (hidden[None], routed[None])


def solution(mesh):
    sizes = mesh.shape
    fine = Mesh(
        mesh.devices.reshape(sizes["ctx"] // 2, 2, 2, sizes["exp"] // 2, sizes["rep"]),
        ("z", "xl", "xh", "y", "rep"),
    )
    placed = (
        P("rep", CTX, EXP, None),
        P("rep", CTX, None),
        P("rep", CTX, EXP),
        P(EXP, None, None),
        P(EXP, None, None),
        P(EXP, None, None),
        P(EXP),
        P(None, EXP),
        P("rep", CTX, None),
        P(CTX + ("rep",), EXP, None),
        P(CTX + ("rep",), EXP, None),
        P(CTX + ("rep",), None, EXP),
    )
    return jax.shard_map(
        body,
        mesh=fine,
        in_specs=placed,
        out_specs=(P("rep", CTX, EXP), P("rep", CTX, EXP)),
        check_vma=False,
    )
```

```python
import jax
import jax.numpy as jnp
from jax import lax
from jax.experimental import pallas as pl
from jax.experimental.pallas import tpu as pltpu
from jax.sharding import Mesh, PartitionSpec as P

score_scale = 192.0 ** (-0.5)
epsilon = 1e-06
never = 1 << 20

f32 = jnp.float32
bf16 = jnp.bfloat16

in_vmem = pl.BlockSpec(memory_space=pltpu.VMEM)
in_smem = pl.BlockSpec(memory_space=pltpu.SMEM)


def iota(shape, dim):
    return lax.broadcasted_iota(jnp.int32, shape, dim)


def dot(a, b, ca, cb, **kw):
    return lax.dot_general(a, b, (((ca,), (cb,)), ((), ())), preferred_element_type=f32, **kw)


def call(kernel, outs, *operands, specs=None, scratch=(), limit=24):
    many = isinstance(outs, list)
    return pl.pallas_call(
        kernel,
        out_shape=outs,
        in_specs=specs or [in_vmem] * len(operands),
        out_specs=[in_vmem] * len(outs) if many else in_vmem,
        scratch_shapes=list(scratch),
        compiler_params=pltpu.CompilerParams(vmem_limit_bytes=limit << 20),
    )(*operands)


def three_terms(x):
    high = x.astype(bf16).astype(f32)
    middle = (x - high).astype(bf16).astype(f32)
    return high, middle, x - high - middle


def repeat_matrix(experts, capacity):
    tall = (experts * capacity, experts)
    return (iota(tall, 0) // capacity == iota(tall, 1)).astype(f32).astype(bf16)


def place_kernel(experts, capacity, routes_ref, place_ref):
    top, rows = routes_ref.shape
    routes = routes_ref[...]
    expert = iota((experts, rows), 0)
    member = routes[0:1] == expert
    for k in range(1, top):
        member = member | (routes[k : k + 1] == expert)
    earlier = (iota((rows, rows), 0) < iota((rows, rows), 1)).astype(f32).astype(bf16)
    count = dot(member.astype(f32).astype(bf16), earlier, 1, 0)
    code = jnp.where(member, count, -1.0).astype(bf16)
    spread = dot(repeat_matrix(experts, capacity), code, 1, 0)
    slot = iota((experts * capacity, rows), 0) % capacity
    place_ref[...] = (spread == slot.astype(f32)).astype(f32).astype(bf16)


def attend_kernel(rows, part_rows, at_ref, key_ref, *refs):
    pair_refs, out_ref, gain_ref = refs[:-2], refs[-2], refs[-1]
    own_block, own_part, own_half, own_y = at_ref[0], at_ref[1], at_ref[2], at_ref[3]
    n_y = len(pair_refs)
    keys = key_ref[...]
    count = keys.shape[0]
    lane = iota((count, 128), 1)
    block = iota((count, 128), 0) // part_rows
    earlier = ((block == lane) & (lane < own_block)).astype(f32).astype(bf16)
    key_row = iota((count, 1), 0)
    is_own = key_row // part_rows == own_block
    own_pos = own_part * part_rows + key_row % part_rows
    both = 2 * rows
    is_first = iota((1, both), 1) < rows
    query_pos = iota((count, both), 1) % rows
    width = gain_ref.shape[2]
    for shift in range(n_y):
        ref = pair_refs[shift]
        pair = jnp.concatenate([ref[0, 0:rows, :], ref[1, 0:rows, :]], axis=0)
        firsts = []
        for half in range(2):
            chosen = dot(earlier, ref[half, rows : rows + 16, width : width + 128], 1, 1)[:, 0:1]
            firsts.append(jnp.where(is_own, own_pos, jnp.where(chosen > 0.5, -1, never)))
        allowed = jnp.where(is_first, firsts[0], firsts[1]) <= query_pos
        scores = dot(keys, pair, 1, 1) * score_scale
        scores = jnp.where(allowed, scores, -1e30)
        top = jnp.max(scores, axis=0, keepdims=True)
        probs = jnp.where(allowed, jnp.exp(scores - top), 0.0)
        total = jnp.sum(probs, axis=0, keepdims=True)
        some = total > 0.0
        scale = jnp.where(some, 1.0 / jnp.where(some, total, 1.0), 0.0)
        latent = dot((probs * scale).astype(bf16), keys, 0, 0).astype(bf16)
        level = jnp.where(some, top + jnp.log(jnp.where(some, total, 1.0)), -1e30)
        terms = three_terms(level)
        at = iota((16, both), 0)
        stats = jnp.zeros((16, both), f32)
        for k, term in enumerate(terms):
            stats = jnp.where(at == k, term, stats)
        stats = stats.astype(bf16)
        for half in range(2):
            head = (own_half ^ half) * n_y + (own_y + n_y - shift) % n_y
            lanes = slice(half * rows, (half + 1) * rows)
            out_ref[head, 0:rows, :] = latent[lanes, :]
            out_ref[head, rows : rows + 16, 0:rows] = stats[:, lanes]
            out_ref[head, rows : rows + 16, rows:] = jnp.zeros((16, keys.shape[1] - rows), bf16)
            gain_ref[head] = ref[half, rows : rows + 16, 0:width]


def project_kernel(rows, part_ref, uv_ref, out_weight_ref, out_ref):
    parts = part_ref.shape[0]
    levels = []
    for s in range(parts):
        stats = part_ref[s, rows : rows + 16, 0:rows].astype(f32)
        levels.append(stats[0:1] + stats[1:2] + stats[2:3])
    top = levels[0]
    for level in levels[1:]:
        top = jnp.maximum(top, level)
    shares = [jnp.exp(level - top) for level in levels]
    total = shares[0]
    for share in shares[1:]:
        total = total + share
    scale = 1.0 / total
    at = iota((rows, rows), 0)
    square = jnp.zeros((rows, rows), f32)
    for s in range(parts):
        square = jnp.where(at == s, shares[s] * scale, square)
    columns = square.T
    latent = columns[:, 0:1] * part_ref[0, 0:rows, :].astype(f32)
    for s in range(1, parts):
        latent = latent + columns[:, s : s + 1] * part_ref[s, 0:rows, :].astype(f32)
    values = dot(latent.astype(bf16), uv_ref[...], 1, 0).astype(bf16)
    width = out_ref.shape[2]
    for d in range(out_ref.shape[0]):
        out_ref[d] = dot(values, out_weight_ref[:, d * width : (d + 1) * width], 1, 0).astype(bf16)


def hidden_kernel(
    part_ref, token_ref, place_ref, router_ref, gain_ref, routes_ref, hidden_ref, rows_ref, pick_ref
):
    attention = part_ref[0].astype(f32)
    for s in range(1, part_ref.shape[0]):
        attention = attention + part_ref[s].astype(f32)
    hidden = (token_ref[...].astype(f32) + attention).astype(bf16)
    hidden_ref[...] = hidden
    rows_ref[...] = dot(place_ref[...], hidden, 1, 0).astype(bf16)
    wide = hidden.astype(f32)
    exact = dict(precision=lax.Precision.HIGHEST)
    scaled = wide * gain_ref[...].astype(f32)
    logits = dot(router_ref[...].astype(f32), scaled, 1, 1, **exact)
    picks = dot(jnp.ones((8, wide.shape[1]), f32), wide * wide, 1, 1, **exact)
    routes = routes_ref[...]
    expert, at = iota(logits.shape, 0), iota(picks.shape, 0)
    for k in range(routes.shape[0]):
        pick = jnp.sum(jnp.where(routes[k : k + 1] == expert, logits, 0.0), axis=0, keepdims=True)
        picks = jnp.where(at == k, pick, picks)
    high, middle, rest = three_terms(picks)
    upper = jnp.concatenate([high, middle], axis=1)
    lower = jnp.concatenate([rest, jnp.zeros_like(rest)], axis=1)
    pick_ref[...] = jnp.concatenate([upper, lower], axis=0).astype(bf16)


def gate_kernel(
    at_ref, own_ref, low_ref, high_ref, far0_ref, far1_ref, gain_ref,
    gate_ref, up_ref, gate2_ref, up2_ref, out_ref, normed_ref,
):
    count, features = normed_ref.shape
    width = own_ref.shape[1]
    half, own_y = at_ref[2], at_ref[3]
    n_y = features // width // 2
    pieces = []
    for shift, first, second in (
        (0, own_ref, own_ref),
        (n_y - 1, low_ref, low_ref),
        (1, high_ref, high_ref),
        (2, far0_ref, far1_ref),
    ):
        y = (own_y + shift) % n_y
        pieces.append((y, first, 0))
        pieces.append((n_y + y, second, second.shape[0] - 32 - count))
    squares = jnp.zeros((count, 1), f32)
    for _, ref, at in pieces:
        wide = ref[at : at + count, :].astype(f32)
        squares = squares + jnp.sum(wide * wide, axis=1, keepdims=True)
    inverse = lax.rsqrt(squares / features + epsilon)
    for s, ref, at in pieces:
        scaled = ref[at : at + count, :].astype(f32) * gain_ref[s][0:1].astype(f32)
        lanes = pl.ds(pl.multiple_of(s * width, 128), width)
        normed_ref[:, lanes] = (scaled * inverse).astype(bf16)
    units = gate_ref.shape[0]
    for a, (g_ref, u_ref) in enumerate(((gate_ref, up_ref), (gate2_ref, up2_ref))):
        pair = jnp.concatenate([g_ref[...], u_ref[...]], axis=0)
        both = dot(pair, normed_ref[...], 1, 1)
        gate, up = both[0:units], both[units:]
        act = (gate / (1.0 + jnp.exp(-gate)) * up).astype(bf16)
        out_ref[pl.ds(pl.multiple_of((half ^ a) * units, 16), units), :] = act


def down_kernel(at_ref, act_ref, down_ref, down2_ref, out_ref, act_all_ref):
    half = at_ref[2]
    n_y, both, _ = act_ref.shape
    units = both // 2
    for x in range(2):
        for y in range(n_y):
            at = (x * n_y + y) * units
            act_all_ref[at : at + units, :] = act_ref[y, x * units : (x + 1) * units, :]
    for a, ref in enumerate((down_ref, down2_ref)):
        out_ref[half ^ a] = dot(act_all_ref[...], ref[...], 0, 0).astype(bf16)


def combine_kernel(experts, capacity, features, routes_ref, place_ref, back_ref, *refs):
    row_refs, out_ref = refs[:-1], refs[-1]
    rows = out_ref.shape[0]
    total = jnp.zeros((8, rows), f32)
    for ref in row_refs:
        for at in range(ref.shape[0] - 32, ref.shape[0], 16):
            terms = ref[at : at + 16, :].astype(f32)
            total = total + (terms[0:8, 0:rows] + terms[0:8, rows:] + terms[8:16, 0:rows])
    routes = routes_ref[...]
    top = routes.shape[0]
    inverse = lax.rsqrt(total[top : top + 1] / features + epsilon)
    gates = 1.0 / (1.0 + jnp.exp(-(inverse * total[0:top])))
    gates = gates / jnp.sum(gates, axis=0, keepdims=True)
    expert = iota((experts, rows), 0)
    weight = jnp.zeros((experts, rows), f32)
    for k in range(top):
        weight = jnp.where(routes[k : k + 1] == expert, gates[k : k + 1], weight)
    high = weight.astype(bf16)
    low = (weight - high.astype(f32)).astype(bf16)
    spread = repeat_matrix(experts, capacity)
    place = place_ref[...].astype(f32)
    back = back_ref[...]
    first = dot((dot(spread, high, 1, 0) * place).astype(bf16), back, 0, 0)
    second = dot((dot(spread, low, 1, 0) * place).astype(bf16), back, 0, 0)
    out_ref[...] = (first + second).astype(bf16)


def shape(*dims, dtype=bf16):
    return jax.ShapeDtypeStruct(dims, dtype)


def swap(x, axes):
    return lax.all_to_all(x, axes, split_axis=0, concat_axis=0, tiled=True)


def copies(x, n):
    return jnp.broadcast_to(x[None], (n,) + x.shape)


def all_shifts(x, n):
    turn = lambda k: [(y, (y + k) % n) for y in range(n)]
    return [x] + [lax.ppermute(x, "y", turn(k)) for k in range(1, n)]


def other_half(x):
    return lax.ppermute(x, "xh", [(0, 1), (1, 0)])


CTX, EXP = ("z", "xl"), ("xh", "y")
OWNERS = CTX + ("rep", "xh")


def body(
    queries,
    latents,
    tokens,
    block_mask,
    uv_weight,
    out_weight,
    norm_gain,
    router_matrix,
    routes,
    gate_weight,
    up_weight,
    down_weight,
):
    rows, latent_width = queries.shape[1], queries.shape[3]
    width = tokens.shape[2]
    experts = router_matrix.shape[0]
    capacity = 4 * rows * routes.shape[2] // (3 * experts)
    blocks = block_mask.shape[1]
    n_exp = lax.axis_size(EXP)
    n_y, n_xh = lax.axis_size("y"), lax.axis_size("xh")
    ctx_place, exp_place = lax.axis_index(CTX), lax.axis_index(EXP)
    half = lax.axis_index("xh")
    part_rows = rows // n_exp
    features = width * n_exp
    slots = experts * capacity
    count = slots // n_xh
    units = gate_weight.shape[1]

    own_keys = lax.dynamic_slice_in_dim(latents[0], exp_place * part_rows, part_rows, 0)
    keys = swap(copies(own_keys, blocks), CTX).reshape(blocks * part_rows, latent_width)
    mask_row = lax.dynamic_index_in_dim(block_mask[0], ctx_place, 0, keepdims=True)
    extra = jnp.concatenate(
        [
            norm_gain[None, :],
            mask_row.astype(bf16),
            jnp.zeros((1, latent_width - width - blocks), bf16),
        ],
        axis=1,
    )
    sent = jnp.concatenate(
        [queries[0, :, 0, :], extra, jnp.zeros((15, latent_width), bf16)], axis=0
    )
    other, gate = lax.optimization_barrier((other_half(sent), gate_weight[0]))
    all_queries = all_shifts(jnp.stack([sent, other]), n_y)

    gate2 = other_half(gate)
    up2 = other_half(up_weight[0])
    down2 = other_half(down_weight[0])

    keys, gate2 = lax.optimization_barrier((keys, gate2))

    routes_t = routes[0].T
    place = call(
        lambda *refs: place_kernel(experts, capacity, *refs), shape(slots, rows), routes_t
    )
    at = jnp.stack([ctx_place, exp_place, half, lax.axis_index("y")]).astype(jnp.int32)
    partial, gains = call(
        lambda *refs: attend_kernel(rows, part_rows, *refs),
        [shape(n_exp, rows + 16, latent_width), shape(n_exp, 16, width)],
        at,
        keys,
        *all_queries,
        specs=[in_smem] + [in_vmem] * (1 + n_y),
    )
    partial = swap(partial, EXP)
    terms = call(
        lambda *refs: project_kernel(rows, *refs),
        shape(n_exp, rows, width),
        partial,
        uv_weight[0],
        out_weight[0],
    )
    terms = swap(terms, EXP)
    hidden, picked, picks = call(
        hidden_kernel,
        [shape(rows, width), shape(slots, width), shape(16, width)],
        terms,
        tokens[0],
        place,
        router_matrix,
        norm_gain[None, :],
        routes_t,
    )
    received = swap(picked.reshape(experts * n_xh, capacity // n_xh, width), OWNERS)
    received, up2 = lax.optimization_barrier((received, up2))
    received = received.reshape(experts, n_xh, capacity // n_xh, width).swapaxes(0, 1)
    mine = jnp.concatenate([received.reshape(slots, width), picks, other_half(picks)], axis=0)
    up_turn = [(y, (y + 1) % n_y) for y in range(n_y)]
    down_turn = [(y, (y + n_y - 1) % n_y) for y in range(n_y)]
    low = lax.ppermute(mine, "y", up_turn)
    high = lax.ppermute(mine, "y", down_turn)
    far0 = lax.ppermute(low[0:count], "y", up_turn)
    far1 = lax.ppermute(high[count:], "y", down_turn)
    far0, far1, down2 = lax.optimization_barrier((far0, far1, down2))
    act = call(
        gate_kernel,
        shape(n_xh * units, count),
        at,
        mine,
        low,
        high,
        far0,
        far1,
        gains,
        gate_weight[0],
        up_weight[0],
        gate2,
        up2,
        specs=[in_smem] + [in_vmem] * 10,
        scratch=[pltpu.VMEM((count, features), bf16)],
    )
    act = swap(copies(act, n_y), "y")
    out = call(
        down_kernel,
        shape(n_xh, count, width),
        at,
        act,
        down_weight[0],
        down2,
        specs=[in_smem] + [in_vmem] * 3,
        scratch=[pltpu.VMEM((n_exp * units, count), bf16)],
    )
    out = out.reshape(n_xh, experts, capacity // n_xh, width).swapaxes(0, 1)
    back = swap(out.reshape(experts * n_xh, capacity // n_xh, width), OWNERS)
    back = back.reshape(slots, width)
    routed = call(
        lambda *refs: combine_kernel(experts, capacity, features, *refs),
        shape(rows, width),
        routes_t,
        place,
        back,
        mine,
        low,
        high,
        far1,
    )
    return (hidden[None], routed[None])


def solution(mesh):
    sizes = mesh.shape
    fine = Mesh(
        mesh.devices.reshape(sizes["ctx"] // 2, 2, 2, sizes["exp"] // 2, sizes["rep"]),
        ("z", "xl", "xh", "y", "rep"),
    )
    placed = (
        P("rep", CTX, EXP, None),
        P("rep", CTX, None),
        P("rep", CTX, EXP),
        P(EXP, None, None),
        P(EXP, None, None),
        P(EXP, None, None),
        P(EXP),
        P(None, EXP),
        P("rep", CTX, None),
        P(CTX + ("rep",), EXP, None),
        P(CTX + ("rep",), EXP, None),
        P(CTX + ("rep",), None, EXP),
    )
    return jax.shard_map(
        body,
        mesh=fine,
        in_specs=placed,
        out_specs=(P("rep", CTX, EXP), P("rep", CTX, EXP)),
        check_vma=False,
    )
```
